32 devices in a mesh: dp: 8 (over z, y), tensor: 4 (over x, core).
Axes of the slice: x: 2, y: 2, z: 4, core: 2. Of those that a mesh axis runs over, the one named last changes fastest.
Arguments:
- hidden_in: bfloat16 [256, 8192], P('dp'), may hold values from -40 to 40
- norm_gain: bfloat16 [8192], P('dp'), may hold values from 0.25 to 2.5
- query_weight: bfloat16 [8192, 8192], P('dp', 'tensor'), may hold values from -0.0625 to 0.0625
- key_weight: bfloat16 [8192, 1024], P('dp', 'tensor'), may hold values from -0.0625 to 0.0625
- value_weight: bfloat16 [8192, 1024], P('dp', 'tensor'), may hold values from -0.0625 to 0.0625
- output_weight: bfloat16 [8192, 8192], P('tensor', 'dp'), may hold values from -0.25 to 0.25
- key_value_cache: bfloat16 [256, 256, 2, 8, 128], P('dp', None, None, 'tensor'), may hold values from -150 to 150, as said below
- cache_lengths: int32 [256], replicated, may hold values from 2 to 256, as said below
- parent_beam: int32 [256], replicated, may hold values from 0 to 255, as said below
- beam_alive: int32 [256], replicated, may hold values 0 or 1
Outputs:
- attention_out: bfloat16 [256, 8192], P(None, 'dp')
The draws below stay inside these ranges and needn't reach their ends.
Inputs may be any that keep to these rules, and one draw needn't show every extreme that they name: `parent_beam`: among the beams of one device, at most 8 have parents that lie on any one device (beam i lies on device i // 32); on every device some device holds exactly 8 of their parents. `cache_lengths`: some beam holds exactly 256 tokens. `key_value_cache`: slots at or past a beam's length hold arbitrary values.
All inputs are finite; a program needn't handle non-finite values.
Results may differ from the reference program's by a relative error of at most 0.012.
Values may be sent and summed in bfloat16 or wider, within the bound.
A program may use at most 128 MiB of HBM per device.

```python
import math
import jax
import jax.numpy as jnp
from jax import lax

D = 8192
HEADS = 64
KV_HEADS = 8
HEAD_DIM = 128
BEAM_DEV = 32
CACHE_LEN = 256
BEAMS = 256
CAP = 8
N_DP = 8


def draw_hidden_in(key, part):
    first_key, second_key, third_key = jax.random.split(key, 3)
    row_scale = jnp.exp(jax.random.uniform(first_key, (BEAMS, 1), jnp.float32, math.log(0.3), math.log(3.0)))
    column_scale = jnp.exp(jax.random.uniform(second_key, (1, D), jnp.float32, math.log(0.3), math.log(3.0)))
    base_values = jnp.clip(jax.random.normal(third_key, (BEAMS, D), jnp.float32), -4.0, 4.0)
    return (base_values * row_scale * column_scale).astype(jnp.bfloat16)


def draw_key_value_cache(key, part):
    first_key = jax.random.fold_in(key, 0)
    full_shape = (BEAMS, CACHE_LEN, 2, KV_HEADS, HEAD_DIM)
    base_values = jnp.clip(jax.random.normal(first_key, full_shape, jnp.float32), -5.0, 5.0)
    return base_values.astype(jnp.bfloat16)


def draw_cache_lengths(key, part):
    first_key, second_key = jax.random.split(key, 2)
    drawn = jax.random.randint(first_key, (BEAMS,), 2, CACHE_LEN + 1)
    longest = jax.random.randint(second_key, (), 0, BEAMS)
    return jnp.where(jnp.arange(BEAMS) == longest, CACHE_LEN, drawn).astype(jnp.int32)


def draw_parent_beam(key, part):

    def one_device(device):
        device_key = jax.random.fold_in(key, device)
        first_key, second_key, third_key = jax.random.split(device_key, 3)
        ordering = jax.random.permutation(first_key, N_DP)
        grouped = ordering[jnp.arange(BEAM_DEV) // CAP]
        shuffled = jax.random.permutation(second_key, grouped)
        within = jax.random.randint(third_key, (BEAM_DEV,), 0, BEAM_DEV)
        return shuffled * BEAM_DEV + within
    return jax.vmap(one_device)(jnp.arange(N_DP)).reshape(-1).astype(jnp.int32)


def set_ends(values, own_key, smallest, high):
    index_at = [jax.random.randint(jax.random.fold_in(own_key, axis), (), 0, length) for axis, length in enumerate(values.shape)]
    main_axis = values.shape.index(max(values.shape))
    beside = index_at[:main_axis] + [(index_at[main_axis] + 1) % values.shape[main_axis]] + index_at[main_axis + 1:]
    return values.at[tuple(index_at)].set(smallest).at[tuple(beside)].set(high)


def levels(stream_key, shape, cuts, least, top_value):
    factor_of, own = 1.0, jax.random.fold_in(stream_key, 6)
    for dim, parts in cuts:
        heights = jnp.exp(jax.random.uniform(jax.random.fold_in(own, dim), (parts,), jnp.float32, least / len(cuts), top_value / len(cuts)))
        factor_of = factor_of * jnp.repeat(heights, shape[dim] // parts).reshape([-1 if axis == dim else 1 for axis in range(len(shape))])
    return factor_of


def bell_draw(own_key, shape, deviation, limit, cuts=(), kind=jnp.bfloat16):
    entries = deviation * jax.random.normal(own_key, shape, jnp.float32)
    if cuts:
        entries = entries * levels(own_key, shape, cuts, -0.22, 0.18)
    return jnp.clip(entries, -limit, limit).astype(kind)


def setup_inputs(seed: int = 0) -> dict:
    keys = jax.random.split(jax.random.key(seed), 11)
    hidden_in = draw_hidden_in(jax.random.fold_in(keys[10], 71), 0)
    norm_gain = jnp.clip(jnp.exp(math.log(2.5) - 2.3025851 * jax.random.uniform(keys[1], (D,), jnp.float32) ** levels(keys[1], (D,), ((0, 8),), -0.2, 0.2)), 0.25, 2.5).astype(jnp.bfloat16)
    query_weight = bell_draw(keys[2], (D, HEADS * HEAD_DIM), D ** -0.5, 0.0625, ((0, 8), (1, 4)))
    key_weight = bell_draw(keys[3], (D, KV_HEADS * HEAD_DIM), D ** -0.5, 0.0625, ((0, 8), (1, 4)))
    value_weight = bell_draw(keys[4], (D, KV_HEADS * HEAD_DIM), D ** -0.5, 0.0625, ((0, 8), (1, 4)))
    output_weight = bell_draw(keys[5], (HEADS * HEAD_DIM, D), (HEADS * HEAD_DIM // 16) ** -0.5, 0.25, ((0, 4), (1, 8)))
    key_value_cache = draw_key_value_cache(jax.random.fold_in(keys[10], 71), 0)
    cache_lengths = draw_cache_lengths(jax.random.fold_in(keys[10], 71), 0)
    parent_beam = draw_parent_beam(jax.random.fold_in(keys[10], 71), 0)
    beam_alive = set_ends((jax.random.randint(keys[9], (BEAMS,), 0, 8) < 7).astype(jnp.int32), jax.random.fold_in(keys[9], 1), 0, 1)
    return {"hidden_in": hidden_in, "norm_gain": norm_gain, "query_weight": query_weight, "key_weight": key_weight, "value_weight": value_weight, "output_weight": output_weight, "key_value_cache": key_value_cache, "cache_lengths": cache_lengths, "parent_beam": parent_beam, "beam_alive": beam_alive}


def rotate(vectors, position):
    half_width = vectors.shape[-1] // 2
    pair_index = jnp.arange(half_width).astype(jnp.float32)
    frequency = jnp.exp(pair_index * (-2.0 * math.log(1000000.0) / vectors.shape[-1]))
    angles = position.astype(jnp.float32)[:, None] * frequency[None, :]
    cosine = jnp.cos(angles)[:, None, :]
    sine_part = jnp.sin(angles)[:, None, :]
    first_half = vectors[..., :half_width]
    second = vectors[..., half_width:]
    return jnp.concatenate([first_half * cosine - second * sine_part, second * cosine + first_half * sine_part], axis=-1)

def attend(queries, key_rows, value_rows, key_new, value_new, length_row):
    row_count, head_total, head_width = queries.shape
    groups = key_rows.shape[2]
    length = key_rows.shape[1]
    grouped = queries.astype(jnp.float32).reshape(row_count, groups, head_total // groups, head_width)
    score_scale = 1.0 / math.sqrt(head_width)
    cached = jnp.einsum('rkgd,rlkd->rkgl', grouped, key_rows.astype(jnp.float32)) * score_scale
    latest = jnp.einsum('rkgd,rkd->rkg', grouped, key_new.astype(jnp.float32)) * score_scale
    is_valid = (jnp.arange(length, dtype=jnp.int32)[None, :] < length_row.astype(jnp.int32)[:, None])[:, None, None, :]
    cached = jnp.where(is_valid, cached, -jnp.inf)
    highest = jnp.maximum(lax.optimization_barrier(jnp.max(cached, axis=-1)), latest)
    cached_exp = jnp.exp(cached - highest[..., None])
    latest_exp = jnp.exp(latest - highest)
    denominator = lax.optimization_barrier(jnp.sum(cached_exp, axis=-1)) + latest_exp
    cached_weight = (cached_exp / denominator[..., None]).astype(jnp.bfloat16)
    latest_weight = (latest_exp / denominator).astype(jnp.bfloat16)
    mixture = jnp.einsum('rkgl,rlkd->rkgd', cached_weight.astype(jnp.float32), value_rows.astype(jnp.float32))
    mixture = mixture + latest_weight.astype(jnp.float32)[..., None] * value_new.astype(jnp.float32)[:, :, None, :]
    return mixture.reshape(row_count, head_total * head_width).astype(jnp.bfloat16)

def reference(hidden_in, norm_gain, query_weight, key_weight, value_weight, output_weight, key_value_cache, cache_lengths, parent_beam, beam_alive):
    hidden_float = hidden_in.astype(jnp.float32)
    inverse = lax.rsqrt(lax.optimization_barrier(jnp.mean(hidden_float * hidden_float, axis=1)) + 1e-06)
    scaled = (hidden_float * norm_gain.astype(jnp.float32)[None, :]).astype(jnp.bfloat16)
    position = jnp.take(cache_lengths, parent_beam)
    query_proj = jnp.dot(scaled, query_weight, preferred_element_type=jnp.float32) * inverse[:, None]
    key_proj = jnp.dot(scaled, key_weight, preferred_element_type=jnp.float32) * inverse[:, None]
    value_proj = jnp.dot(scaled, value_weight, preferred_element_type=jnp.float32) * inverse[:, None]
    queries = rotate(query_proj.reshape(BEAMS, HEADS, HEAD_DIM), position).astype(jnp.bfloat16)
    key_new = rotate(key_proj.reshape(BEAMS, KV_HEADS, HEAD_DIM), position).astype(jnp.bfloat16)
    value_new = value_proj.reshape(BEAMS, KV_HEADS, HEAD_DIM).astype(jnp.bfloat16)

    def one_beam(beam_items):
        query_row, key_row, value_row, parent_row, alive_row = beam_items
        cache_block = lax.dynamic_index_in_dim(key_value_cache, parent_row, 0, keepdims=True)
        length_one = lax.dynamic_index_in_dim(cache_lengths, parent_row, 0, keepdims=True)
        mixture = attend(query_row[None], cache_block[:, :, 0], cache_block[:, :, 1], key_row[None], value_row[None], length_one)
        return jnp.where(alive_row > 0, mixture[0], jnp.zeros_like(mixture[0]))
    attention = lax.map(one_beam, (queries, key_new, value_new, parent_beam, beam_alive))
    return jnp.dot(attention, output_weight, preferred_element_type=jnp.float32).astype(jnp.bfloat16)
```

```python
import functools
import math

import jax
import jax.numpy as jnp
from jax import lax
from jax.experimental import pallas as pl
from jax.experimental.pallas import tpu as pltpu
from jax.sharding import PartitionSpec as P

HEAD_DIM = 128


def rotate(vectors, position):
    half_width = vectors.shape[-1] // 2
    pair_index = jnp.arange(half_width).astype(jnp.float32)
    frequency = jnp.exp(pair_index * (-2.0 * math.log(1000000.0) / vectors.shape[-1]))
    angles = position.astype(jnp.float32)[:, None] * frequency[None, :]
    cosine = jnp.cos(angles)[:, None, :]
    sine_part = jnp.sin(angles)[:, None, :]
    first_half = vectors[..., :half_width]
    second = vectors[..., half_width:]
    return jnp.concatenate(
        [first_half * cosine - second * sine_part, second * cosine + first_half * sine_part],
        axis=-1,
    )


def attend_kernel(capacity, head_count, parent_ref, length_ref, new_ref, cache_ref, out_ref):
    groups = cache_ref.shape[2]
    length = cache_ref.shape[3]
    per_group = head_count // groups
    first = pl.program_id(0) * capacity
    score_scale = 1.0 / math.sqrt(HEAD_DIM)
    rows = groups * per_group
    scores, latest, limits = [], [], []
    for slot in range(capacity):
        parent = parent_ref[first + slot]
        limits.append(jnp.full((rows, 1), length_ref[first + slot], jnp.int32))
        for group in range(groups):
            query = new_ref[0, slot, group * per_group : (group + 1) * per_group, :]
            key_row = new_ref[0, slot, head_count + group : head_count + group + 1, :]
            keys = cache_ref[parent, 0, group]
            scores.append(
                lax.dot_general(
                    query, keys, (((1,), (1,)), ((), ())), preferred_element_type=jnp.float32
                )
            )
            latest.append(
                jnp.sum(
                    query.astype(jnp.float32) * key_row.astype(jnp.float32), axis=1, keepdims=True
                )
            )
    cached = jnp.concatenate(scores, axis=0) * score_scale
    newest = jnp.concatenate(latest, axis=0) * score_scale
    limit = jnp.concatenate(limits, axis=0)
    slots = lax.broadcasted_iota(jnp.int32, cached.shape, 1)
    cached = jnp.where(slots < limit, cached, -jnp.inf)
    highest = jnp.maximum(jnp.max(cached, axis=1, keepdims=True), newest)
    cached_exp = jnp.exp(cached - highest)
    newest_exp = jnp.exp(newest - highest)
    denominator = jnp.sum(cached_exp, axis=1, keepdims=True) + newest_exp
    weight = (cached_exp / denominator).astype(jnp.bfloat16)
    newest_weight = (newest_exp / denominator).astype(jnp.bfloat16).astype(jnp.float32)
    for slot in range(capacity):
        parent = parent_ref[first + slot]
        parts = []
        for group in range(groups):
            low = (slot * groups + group) * per_group
            values = cache_ref[parent, 1, group]
            value_row = new_ref[
                0, slot, head_count + groups + group : head_count + groups + group + 1, :
            ]
            mixed = jnp.dot(
                weight[low : low + per_group], values, preferred_element_type=jnp.float32
            )
            mixed = mixed + newest_weight[low : low + per_group] * value_row.astype(jnp.float32)
            parts.append(mixed)
        out_ref[0, slot] = jnp.concatenate(parts, axis=0).astype(jnp.bfloat16)


def attend(parents, lengths, arrived, cache, head_count):
    device_count, capacity, rows, _ = arrived.shape
    whole = cache.shape
    spec = pltpu.PrefetchScalarGridSpec(
        num_scalar_prefetch=2,
        grid=(device_count,),
        in_specs=[
            pl.BlockSpec((1, capacity, rows, HEAD_DIM), lambda i, *_: (i, 0, 0, 0)),
            pl.BlockSpec(whole, lambda i, *_: (0, 0, 0, 0, 0)),
        ],
        out_specs=pl.BlockSpec((1, capacity, head_count, HEAD_DIM), lambda i, *_: (i, 0, 0, 0)),
    )
    return pl.pallas_call(
        functools.partial(attend_kernel, capacity, head_count),
        grid_spec=spec,
        out_shape=jax.ShapeDtypeStruct(
            (device_count, capacity, head_count, HEAD_DIM), jnp.bfloat16
        ),
        compiler_params=pltpu.CompilerParams(vmem_limit_bytes=40 * 1024 * 1024),
        name="attend",
    )(parents, lengths, arrived, cache)


def arrival_ranks(sources):
    ordinal = jnp.arange(sources.shape[-1], dtype=jnp.int32)
    earlier = (sources[..., None, :] == sources[..., :, None]) & (
        ordinal[None, :] < ordinal[:, None]
    )
    return jnp.sum(earlier.astype(jnp.int32), axis=-1)


def body(
    hidden_in,
    norm_gain,
    query_weight,
    key_weight,
    value_weight,
    output_weight,
    key_value_cache,
    cache_lengths,
    parent_beam,
    beam_alive,
):
    device_count = lax.axis_size("dp")
    device_rank = lax.axis_index("dp")
    local_beams = hidden_in.shape[0]
    capacity = max(2, (2 * local_beams + device_count - 1) // device_count)
    slot_total = device_count * capacity
    query_width = query_weight.shape[1]
    key_width = key_weight.shape[1]
    head_count = query_width // HEAD_DIM
    group_count = key_width // HEAD_DIM
    row_count = head_count + 2 * group_count

    cache = jnp.transpose(key_value_cache, (0, 2, 3, 1, 4))

    all_parents = parent_beam.reshape(device_count, local_beams)
    all_sources = all_parents // local_beams
    all_ranks = arrival_ranks(all_sources)
    beam_index = jnp.arange(parent_beam.shape[0], dtype=jnp.int32)
    all_positions = jnp.sum(
        jnp.where(parent_beam[:, None] == beam_index[None, :], cache_lengths[None, :], 0), axis=1
    )
    held = (all_sources == device_rank)[:, None, :] & (
        all_ranks[:, None, :] == jnp.arange(capacity, dtype=jnp.int32)[None, :, None]
    )
    slot_parent = jnp.sum(jnp.where(held, (all_parents % local_beams)[:, None, :], 0), axis=2)
    slot_length = jnp.sum(
        jnp.where(held, all_positions.reshape(device_count, 1, local_beams), 0), axis=2
    )

    first_beam = device_rank * local_beams
    my_alive = lax.dynamic_slice_in_dim(beam_alive, first_beam, local_beams)
    position = lax.dynamic_slice_in_dim(all_positions, first_beam, local_beams)
    my_source = lax.dynamic_slice_in_dim(all_sources, device_rank, 1)[0]
    my_rank = lax.dynamic_slice_in_dim(all_ranks, device_rank, 1)[0]
    target = my_source * capacity + my_rank
    placing = (jnp.arange(slot_total, dtype=jnp.int32)[:, None] == target[None, :]).astype(
        jnp.bfloat16
    )
    picking = (
        (jnp.arange(slot_total, dtype=jnp.int32)[None, :] == target[:, None])
        & (my_alive[:, None] > 0)
    ).astype(jnp.bfloat16)

    hidden_float = hidden_in.astype(jnp.float32)
    inverse = lax.rsqrt(jnp.mean(hidden_float * hidden_float, axis=1) + 1e-06)
    blocked = lax.all_to_all(hidden_in, "dp", split_axis=1, concat_axis=0, tiled=True)
    scaled = (blocked.astype(jnp.float32) * norm_gain.astype(jnp.float32)[None, :]).astype(
        jnp.bfloat16
    )
    partial = jnp.concatenate(
        [
            jnp.dot(scaled, weight, preferred_element_type=jnp.float32).astype(jnp.bfloat16)
            for weight in (query_weight, key_weight, value_weight)
        ],
        axis=1,
    ).reshape(device_count, local_beams, query_width + 2 * key_width)
    partial = lax.all_to_all(partial, "dp", split_axis=0, concat_axis=0, tiled=True)
    summed = jnp.sum(partial.astype(jnp.float32), axis=0) * inverse[:, None]
    heads = summed.reshape(local_beams, row_count, HEAD_DIM)
    turned = rotate(heads[:, : head_count + group_count], position)
    fresh = jnp.concatenate([turned, heads[:, head_count + group_count :]], axis=1).astype(
        jnp.bfloat16
    )
    packed = jnp.dot(
        placing, fresh.reshape(local_beams, row_count * HEAD_DIM), preferred_element_type=jnp.float32
    ).astype(jnp.bfloat16)
    arrived = lax.all_to_all(
        packed.reshape(device_count, capacity, row_count, HEAD_DIM),
        "dp",
        split_axis=0,
        concat_axis=0,
        tiled=True,
    )
    mixed = attend(
        slot_parent.reshape(-1), slot_length.reshape(-1), arrived, cache, head_count
    )
    back = lax.all_to_all(mixed, "dp", split_axis=0, concat_axis=0, tiled=True)
    attention = jnp.dot(
        picking, back.reshape(slot_total, query_width), preferred_element_type=jnp.float32
    ).astype(jnp.bfloat16)
    gathered = lax.all_to_all(
        jnp.broadcast_to(attention[None], (device_count,) + attention.shape),
        "dp",
        split_axis=0,
        concat_axis=0,
        tiled=True,
    ).reshape(device_count * local_beams, query_width)
    partial_sum = jnp.dot(gathered, output_weight, preferred_element_type=jnp.float32)
    return lax.psum(partial_sum, "tensor").astype(jnp.bfloat16)


def solution(mesh):
    placed = (
        P("dp", None),
        P("dp"),
        P("dp", "tensor"),
        P("dp", "tensor"),
        P("dp", "tensor"),
        P("tensor", "dp"),
        P("dp", None, None, "tensor", None),
        P(),
        P(),
        P(),
    )
    return jax.shard_map(body, mesh=mesh, in_specs=placed, out_specs=P(None, "dp"), check_vma=False)
```

```python
import functools
import math

import jax
import jax.numpy as jnp
from jax import lax
from jax.experimental import pallas as pl
from jax.experimental.pallas import tpu as pltpu
from jax.sharding import PartitionSpec as P

HEAD_DIM = 128


def turn_angles(position):
    half_width = HEAD_DIM // 2
    pair_index = jnp.arange(half_width).astype(jnp.float32)
    frequency = jnp.exp(pair_index * (-2.0 * math.log(1000000.0) / HEAD_DIM))
    angles = position.astype(jnp.float32)[:, None] * frequency[None, :]
    cosine, sine = jnp.cos(angles), jnp.sin(angles)
    return (
        jnp.concatenate([cosine, cosine], axis=1),
        jnp.concatenate([-sine, sine], axis=1),
    )


def attend_kernel(capacity, head_count, parent_ref, length_ref, new_ref, cache_ref, out_ref):
    groups = cache_ref.shape[2]
    length = cache_ref.shape[3]
    per_group = head_count // groups
    first = pl.program_id(0) * capacity
    score_scale = 1.0 / math.sqrt(HEAD_DIM)
    rows = groups * per_group
    scores, latest, limits = [], [], []
    for slot in range(capacity):
        parent = parent_ref[first + slot]
        limits.append(jnp.full((rows, 1), length_ref[first + slot], jnp.int32))
        for group in range(groups):
            query = new_ref[0, slot, group * per_group : (group + 1) * per_group, :]
            key_row = new_ref[0, slot, head_count + group : head_count + group + 1, :]
            keys = cache_ref[parent, 0, group]
            scores.append(
                lax.dot_general(
                    query, keys, (((1,), (1,)), ((), ())), preferred_element_type=jnp.float32
                )
            )
            latest.append(
                jnp.sum(
                    query.astype(jnp.float32) * key_row.astype(jnp.float32), axis=1, keepdims=True
                )
            )
    cached = jnp.concatenate(scores, axis=0) * score_scale
    newest = jnp.concatenate(latest, axis=0) * score_scale
    limit = jnp.concatenate(limits, axis=0)
    slots = lax.broadcasted_iota(jnp.int32, cached.shape, 1)
    cached = jnp.where(slots < limit, cached, -jnp.inf)
    highest = jnp.maximum(jnp.max(cached, axis=1, keepdims=True), newest)
    cached_exp = jnp.exp(cached - highest)
    newest_exp = jnp.exp(newest - highest)
    denominator = jnp.sum(cached_exp, axis=1, keepdims=True) + newest_exp
    weight = (cached_exp / denominator).astype(jnp.bfloat16)
    newest_weight = (newest_exp / denominator).astype(jnp.bfloat16).astype(jnp.float32)
    for slot in range(capacity):
        parent = parent_ref[first + slot]
        parts = []
        for group in range(groups):
            low = (slot * groups + group) * per_group
            values = cache_ref[parent, 1, group]
            value_row = new_ref[
                0, slot, head_count + groups + group : head_count + groups + group + 1, :
            ]
            mixed = jnp.dot(
                weight[low : low + per_group], values, preferred_element_type=jnp.float32
            )
            mixed = mixed + newest_weight[low : low + per_group] * value_row.astype(jnp.float32)
            parts.append(mixed)
        out_ref[0, slot] = jnp.concatenate(parts, axis=0).astype(jnp.bfloat16)


def attend(parents, lengths, arrived, cache, head_count):
    device_count, capacity, rows, _ = arrived.shape
    whole = cache.shape
    spec = pltpu.PrefetchScalarGridSpec(
        num_scalar_prefetch=2,
        grid=(device_count,),
        in_specs=[
            pl.BlockSpec((1, capacity, rows, HEAD_DIM), lambda i, *_: (i, 0, 0, 0)),
            pl.BlockSpec(whole, lambda i, *_: (0, 0, 0, 0, 0)),
        ],
        out_specs=pl.BlockSpec((1, capacity, head_count, HEAD_DIM), lambda i, *_: (i, 0, 0, 0)),
    )
    return pl.pallas_call(
        functools.partial(attend_kernel, capacity, head_count),
        grid_spec=spec,
        out_shape=jax.ShapeDtypeStruct(
            (device_count, capacity, head_count, HEAD_DIM), jnp.bfloat16
        ),
        compiler_params=pltpu.CompilerParams(vmem_limit_bytes=40 * 1024 * 1024),
        name="attend",
    )(parents, lengths, arrived, cache)


MESH = pl.DeviceIdType.MESH


def remote(src, dst, send_sem, recv_sem, device):
    return pltpu.make_async_remote_copy(
        src_ref=src,
        dst_ref=dst,
        send_sem=send_sem,
        recv_sem=recv_sem,
        device_id=device,
        device_id_type=MESH,
    )


def greet(devices):
    barrier = pltpu.get_barrier_semaphore()
    for device in devices:
        pl.semaphore_signal(barrier, inc=1, device_id=device, device_id_type=MESH)
    pl.semaphore_wait(barrier, len(devices))


def scatter_sum(chunk, high, low, partner, peers, bufs):
    product, half, got, block, landed, sems = bufs
    half_send, half_recv, block_send, block_recv = sems
    half[chunk] = product[chunk, :, 1 - low].astype(jnp.bfloat16)
    first = remote(
        half.at[chunk], got.at[chunk], half_send.at[chunk], half_recv.at[chunk], partner
    )
    first.start()

    def second():
        first.wait()
        copies = []
        for step, peer in enumerate(peers):
            other = lax.rem(high + step + 1, len(peers) + 1)
            block[chunk, step] = (
                product[chunk, other, low] + got[chunk, other].astype(jnp.float32)
            ).astype(jnp.bfloat16)
            copy = remote(
                block.at[chunk, step],
                landed.at[chunk, step],
                block_send.at[chunk, step],
                block_recv.at[chunk, step],
                peer,
            )
            copy.start()
            copies.append(copy)

        def finish():
            for copy in copies:
                copy.wait()
            total = product[chunk, high, low] + got[chunk, high].astype(jnp.float32)
            for step in range(len(peers)):
                total = total + landed[chunk, step].astype(jnp.float32)
            return total

        return finish

    return second


def project_kernel(
    n,
    hidden_ref,
    gain_ref,
    query_ref,
    key_ref,
    value_ref,
    cosine_ref,
    sine_ref,
    out_ref,
    blocks,
    product,
    half,
    got,
    block,
    landed,
    move_send,
    move_recv,
    pass_send,
    pass_recv,
    half_send,
    half_recv,
    block_send,
    block_recv,
):
    me = lax.axis_index("dp")
    rank = lax.axis_index("tensor")
    core = lax.rem(rank, 2)
    twin = (me, rank + 1 - 2 * core)
    high, low = me // 2, lax.rem(me, 2)
    partner = (me + 1 - 2 * low, rank)
    peers = [(lax.rem(high + d, n // 2) * 2 + low, rank) for d in range(1, n // 2)]
    others = [(lax.rem(me + d, n), rank) for d in range(1, n)]
    rows, depth = hidden_ref.shape[0], query_ref.shape[0]
    part = rows // 2
    greet(others + [twin])
    mine = pl.ds(pl.multiple_of(core * part, part), part)
    theirs = pl.ds(pl.multiple_of((1 - core) * part, part), part)
    moves = []
    for d in range(1, n):
        target = lax.rem(me + d, n)
        columns = pl.ds(pl.multiple_of(target * depth, depth), depth)
        copy = remote(
            hidden_ref.at[mine, columns],
            blocks.at[d, mine],
            move_send.at[d],
            move_recv.at[d],
            (target, rank),
        )
        copy.start()
        moves.append(copy)
    blocks[0] = hidden_ref[:, pl.ds(pl.multiple_of(me * depth, depth), depth)]
    hidden = hidden_ref[...].astype(jnp.float32)
    inverse = lax.rsqrt(
        jnp.sum(hidden * hidden, axis=1, keepdims=True) / hidden_ref.shape[1] + 1e-06
    )
    passes = []
    for d in range(1, n):
        moves[d - 1].wait_recv()
        copy = remote(
            blocks.at[d, mine], blocks.at[d, mine], pass_send.at[d], pass_recv.at[d], twin
        )
        copy.start()
        passes.append(copy)
    for d in range(1, n):
        moves[d - 1].wait_send()
        passes[d - 1].wait_send()
        remote(
            blocks.at[d, theirs], blocks.at[d, theirs], pass_send.at[d], pass_recv.at[d], twin
        ).wait_recv()
    gain = gain_ref[...].astype(jnp.float32)
    scaled = jnp.concatenate(
        [(blocks[d].astype(jnp.float32) * gain).astype(jnp.bfloat16) for d in range(n)], axis=0
    )
    width = product.shape[-1]
    chunks = product.shape[0]
    bufs = (product, half, got, block, landed, (half_send, half_recv, block_send, block_recv))
    seconds = []
    for chunk in range(chunks):
        if chunk < chunks - 1:
            weight = query_ref[:, chunk * width : (chunk + 1) * width]
        else:
            weight = jnp.concatenate([key_ref[...], value_ref[...]], axis=1)
        result = jnp.dot(scaled, weight, preferred_element_type=jnp.float32)
        for d in range(n):
            owner = lax.rem(me - d + n, n)
            product[chunk, owner // 2, lax.rem(owner, 2)] = result[d * rows : (d + 1) * rows]
        seconds.append(scatter_sum(chunk, high, low, partner, peers, bufs))
    finishes = [second() for second in seconds]
    cosine, sine = cosine_ref[...], sine_ref[...]
    for chunk in range(chunks):
        total = finishes[chunk]() * inverse
        for first in range(0, width, HEAD_DIM):
            vector = total[:, first : first + HEAD_DIM]
            if chunk < chunks - 1 or first < width // 2:
                vector = vector * cosine + pltpu.roll(vector, HEAD_DIM // 2, 1) * sine
            at = chunk * width + first
            out_ref[:, at : at + HEAD_DIM] = vector.astype(jnp.bfloat16)


def sum_scratch(chunks, nh, rows, width):
    return [
        pltpu.VMEM((chunks, nh, 2, rows, width), jnp.float32),
        pltpu.VMEM((chunks, nh, rows, width), jnp.bfloat16),
        pltpu.VMEM((chunks, nh, rows, width), jnp.bfloat16),
        pltpu.VMEM((chunks, max(nh - 1, 1), rows, width), jnp.bfloat16),
        pltpu.VMEM((chunks, max(nh - 1, 1), rows, width), jnp.bfloat16),
    ]


def sum_sems(chunks, nh):
    return [
        pltpu.SemaphoreType.DMA((chunks,)),
        pltpu.SemaphoreType.DMA((chunks,)),
        pltpu.SemaphoreType.DMA((chunks, max(nh - 1, 1))),
        pltpu.SemaphoreType.DMA((chunks, max(nh - 1, 1))),
    ]


def project(n, hidden, gain, query_weight, key_weight, value_weight, cosine, sine):
    rows = hidden.shape[0]
    depth, query_width = query_weight.shape
    width = 2 * key_weight.shape[1]
    chunks = query_width // width + 1
    vmem = pl.BlockSpec(memory_space=pltpu.VMEM)
    return pl.pallas_call(
        functools.partial(project_kernel, n),
        out_shape=jax.ShapeDtypeStruct((rows, chunks * width), jnp.bfloat16),
        in_specs=[vmem] * 7,
        out_specs=vmem,
        scratch_shapes=[pltpu.VMEM((n, rows, depth), jnp.bfloat16)]
        + sum_scratch(chunks, n // 2, rows, width)
        + [pltpu.SemaphoreType.DMA((n,))] * 4
        + sum_sems(chunks, n // 2),
        compiler_params=pltpu.CompilerParams(
            collective_id=0, has_side_effects=True, vmem_limit_bytes=40 * 1024 * 1024
        ),
        cost_estimate=pl.CostEstimate(
            flops=2 * n * rows * depth * chunks * width, bytes_accessed=8000000, transcendentals=0
        ),
        name="project",
    )(hidden, gain, query_weight, key_weight, value_weight, cosine, sine)


def output_kernel(
    n,
    ranks,
    mixed_ref,
    weight_ref,
    out_ref,
    gathered,
    whole,
    product,
    half,
    got,
    block,
    landed,
    own_send,
    pass_send,
    take_recv,
    end_send,
    end_pass,
    end_recv,
    half_send,
    half_recv,
    block_send,
    block_recv,
):
    me = lax.axis_index("dp")
    rank = lax.axis_index("tensor")
    high, low = me // 2, lax.rem(me, 2)
    partner = (me + 1 - 2 * low, rank)
    nh = n // 2
    row_peers = [(lax.rem(high + d, nh) * 2 + low, rank) for d in range(1, nh)]
    x, core = rank // 2, lax.rem(rank, 2)
    twin = (me, rank + 1 - 2 * core)
    nx = ranks // 2
    x_peers = [(me, lax.rem(x + d, nx) * 2 + core) for d in range(1, nx)]
    greet([partner, twin] + row_peers + x_peers)

    sends = []
    for d, peer in enumerate([partner] + row_peers):
        copy = remote(mixed_ref, gathered.at[me], own_send.at[d], take_recv.at[me], peer)
        copy.start()
        sends.append(copy)
    gathered[me] = mixed_ref[...]
    for d in range(1, nh):
        source = lax.rem(high - d + nh, nh) * 2 + low
        spot = gathered.at[source]
        remote(spot, spot, own_send.at[d], take_recv.at[source], partner).wait_recv()
        copy = remote(spot, spot, pass_send.at[d], take_recv.at[source], partner)
        copy.start()
        sends.append(copy)
    for d in range(nh):
        source = lax.rem(high - d + nh, nh) * 2 + 1 - low
        spot = gathered.at[source]
        remote(spot, spot, own_send.at[0], take_recv.at[source], partner).wait_recv()
    for copy in sends:
        copy.wait_send()

    rows, width = product.shape[3], product.shape[4]
    chunks = product.shape[0]
    everything = gathered[...].reshape(n * mixed_ref.shape[0], mixed_ref.shape[1])
    bufs = (product, half, got, block, landed, (half_send, half_recv, block_send, block_recv))
    seconds = []
    for chunk in range(chunks):
        result = jnp.dot(
            everything,
            weight_ref[:, chunk * width : (chunk + 1) * width],
            preferred_element_type=jnp.float32,
        )
        for place in range(ranks):
            product[chunk, place // 2, place % 2] = result[place * rows : (place + 1) * rows]
        seconds.append(scatter_sum(chunk, x, core, twin, x_peers, bufs))
    finishes = [second() for second in seconds]
    sends = []
    for chunk in range(chunks):
        whole[chunk, rank] = finishes[chunk]().astype(jnp.bfloat16)
        spot = whole.at[chunk, rank]
        for d, peer in enumerate([twin] + x_peers):
            copy = remote(spot, spot, end_send.at[chunk, d], end_recv.at[chunk, rank], peer)
            copy.start()
            sends.append(copy)
    for chunk in range(chunks):
        for d in range(1, nx):
            source = lax.rem(x - d + nx, nx) * 2 + core
            spot = whole.at[chunk, source]
            remote(
                spot, spot, end_send.at[chunk, d], end_recv.at[chunk, source], twin
            ).wait_recv()
            copy = remote(
                spot, spot, end_pass.at[chunk, d], end_recv.at[chunk, source], twin
            )
            copy.start()
            sends.append(copy)
    for chunk in range(chunks):
        for d in range(nx):
            source = lax.rem(x - d + nx, nx) * 2 + 1 - core
            spot = whole.at[chunk, source]
            remote(
                spot, spot, end_send.at[chunk, 0], end_recv.at[chunk, source], twin
            ).wait_recv()
    for copy in sends:
        copy.wait_send()
    for chunk in range(chunks):
        for place in range(ranks):
            out_ref[place * rows : (place + 1) * rows, chunk * width : (chunk + 1) * width] = whole[
                chunk, place
            ]


def output(n, ranks, mixed, weight):
    local, depth = mixed.shape
    columns = weight.shape[1]
    width = min(256, columns)
    chunks = columns // width
    rows = n * local // ranks
    vmem = pl.BlockSpec(memory_space=pltpu.VMEM)
    return pl.pallas_call(
        functools.partial(output_kernel, n, ranks),
        out_shape=jax.ShapeDtypeStruct((n * local, columns), jnp.bfloat16),
        in_specs=[vmem] * 2,
        out_specs=vmem,
        scratch_shapes=[
            pltpu.VMEM((n, local, depth), jnp.bfloat16),
            pltpu.VMEM((chunks, ranks, rows, width), jnp.bfloat16),
        ]
        + sum_scratch(chunks, ranks // 2, rows, width)
        + [pltpu.SemaphoreType.DMA((n,))] * 3
        + [pltpu.SemaphoreType.DMA((chunks, ranks))] * 3
        + sum_sems(chunks, ranks // 2),
        compiler_params=pltpu.CompilerParams(
            collective_id=1, has_side_effects=True, vmem_limit_bytes=40 * 1024 * 1024
        ),
        cost_estimate=pl.CostEstimate(
            flops=2 * n * local * depth * columns, bytes_accessed=8000000, transcendentals=0
        ),
        name="output",
    )(mixed, weight)


def arrival_ranks(sources):
    ordinal = jnp.arange(sources.shape[-1], dtype=jnp.int32)
    earlier = (sources[..., None, :] == sources[..., :, None]) & (
        ordinal[None, :] < ordinal[:, None]
    )
    return jnp.sum(earlier.astype(jnp.int32), axis=-1)


def body(
    hidden_in,
    norm_gain,
    query_weight,
    key_weight,
    value_weight,
    output_weight,
    key_value_cache,
    cache_lengths,
    parent_beam,
    beam_alive,
):
    device_count = lax.axis_size("dp")
    device_rank = lax.axis_index("dp")
    local_beams = hidden_in.shape[0]
    capacity = max(2, (2 * local_beams + device_count - 1) // device_count)
    slot_total = device_count * capacity
    query_width = query_weight.shape[1]
    key_width = key_weight.shape[1]
    head_count = query_width // HEAD_DIM
    group_count = key_width // HEAD_DIM
    row_count = head_count + 2 * group_count

    cache = jnp.transpose(key_value_cache, (0, 2, 3, 1, 4))

    all_parents = parent_beam.reshape(device_count, local_beams)
    all_sources = all_parents // local_beams
    all_ranks = arrival_ranks(all_sources)
    beam_index = jnp.arange(parent_beam.shape[0], dtype=jnp.int32)
    all_positions = jnp.sum(
        jnp.where(parent_beam[:, None] == beam_index[None, :], cache_lengths[None, :], 0), axis=1
    )
    held = (all_sources == device_rank)[:, None, :] & (
        all_ranks[:, None, :] == jnp.arange(capacity, dtype=jnp.int32)[None, :, None]
    )
    slot_parent = jnp.sum(jnp.where(held, (all_parents % local_beams)[:, None, :], 0), axis=2)
    slot_length = jnp.sum(
        jnp.where(held, all_positions.reshape(device_count, 1, local_beams), 0), axis=2
    )

    first_beam = device_rank * local_beams
    my_alive = lax.dynamic_slice_in_dim(beam_alive, first_beam, local_beams)
    position = lax.dynamic_slice_in_dim(all_positions, first_beam, local_beams)
    my_source = lax.dynamic_slice_in_dim(all_sources, device_rank, 1)[0]
    my_rank = lax.dynamic_slice_in_dim(all_ranks, device_rank, 1)[0]
    target = my_source * capacity + my_rank
    placing = (jnp.arange(slot_total, dtype=jnp.int32)[:, None] == target[None, :]).astype(
        jnp.bfloat16
    )
    picking = (
        (jnp.arange(slot_total, dtype=jnp.int32)[None, :] == target[:, None])
        & (my_alive[:, None] > 0)
    ).astype(jnp.bfloat16)

    cosine, sine = turn_angles(position)
    fresh = project(
        device_count,
        hidden_in,
        norm_gain[None, :],
        query_weight,
        key_weight,
        value_weight,
        cosine,
        sine,
    )
    packed = jnp.dot(
        placing, fresh, preferred_element_type=jnp.float32
    ).astype(jnp.bfloat16)
    arrived = lax.all_to_all(
        packed.reshape(device_count, capacity, row_count, HEAD_DIM),
        "dp",
        split_axis=0,
        concat_axis=0,
        tiled=True,
    )
    mixed = attend(
        slot_parent.reshape(-1), slot_length.reshape(-1), arrived, cache, head_count
    )
    back = lax.all_to_all(mixed, "dp", split_axis=0, concat_axis=0, tiled=True)
    attention = jnp.dot(
        picking, back.reshape(slot_total, query_width), preferred_element_type=jnp.float32
    ).astype(jnp.bfloat16)
    return output(device_count, lax.axis_size("tensor"), attention, output_weight)


def solution(mesh):
    placed = (
        P("dp", None),
        P("dp"),
        P("dp", "tensor"),
        P("dp", "tensor"),
        P("dp", "tensor"),
        P("tensor", "dp"),
        P("dp", None, None, "tensor", None),
        P(),
        P(),
        P(),
    )
    return jax.shard_map(body, mesh=mesh, in_specs=placed, out_specs=P(None, "dp"), check_vma=False)
```

```python
import functools
import math

import jax
import jax.numpy as jnp
from jax import lax
from jax.experimental import pallas as pl
from jax.experimental.pallas import tpu as pltpu
from jax.sharding import PartitionSpec as P

HEAD_DIM = 128


def turn_angles(position):
    half_width = HEAD_DIM // 2
    pair_index = jnp.arange(half_width).astype(jnp.float32)
    frequency = jnp.exp(pair_index * (-2.0 * math.log(1000000.0) / HEAD_DIM))
    angles = position.astype(jnp.float32)[:, None] * frequency[None, :]
    cosine, sine = jnp.cos(angles), jnp.sin(angles)
    return (
        jnp.concatenate([cosine, cosine], axis=1),
        jnp.concatenate([-sine, sine], axis=1),
    )


def attend_kernel(capacity, head_count, parent_ref, length_ref, new_ref, cache_ref, out_ref):
    groups = cache_ref.shape[2]
    length = cache_ref.shape[3]
    per_group = head_count // groups
    first = pl.program_id(0) * capacity
    score_scale = 1.0 / math.sqrt(HEAD_DIM)
    rows = groups * per_group
    scores, latest, limits = [], [], []
    for slot in range(capacity):
        parent = parent_ref[first + slot]
        limits.append(jnp.full((rows, 1), length_ref[first + slot], jnp.int32))
        for group in range(groups):
            query = new_ref[0, slot, group * per_group : (group + 1) * per_group, :]
            key_row = new_ref[0, slot, head_count + group : head_count + group + 1, :]
            keys = cache_ref[parent, 0, group]
            scores.append(
                lax.dot_general(
                    query, keys, (((1,), (1,)), ((), ())), preferred_element_type=jnp.float32
                )
            )
            latest.append(
                jnp.sum(
                    query.astype(jnp.float32) * key_row.astype(jnp.float32), axis=1, keepdims=True
                )
            )
    cached = jnp.concatenate(scores, axis=0) * score_scale
    newest = jnp.concatenate(latest, axis=0) * score_scale
    limit = jnp.concatenate(limits, axis=0)
    slots = lax.broadcasted_iota(jnp.int32, cached.shape, 1)
    cached = jnp.where(slots < limit, cached, -jnp.inf)
    highest = jnp.maximum(jnp.max(cached, axis=1, keepdims=True), newest)
    cached_exp = jnp.exp(cached - highest)
    newest_exp = jnp.exp(newest - highest)
    denominator = jnp.sum(cached_exp, axis=1, keepdims=True) + newest_exp
    weight = (cached_exp / denominator).astype(jnp.bfloat16)
    newest_weight = (newest_exp / denominator).astype(jnp.bfloat16).astype(jnp.float32)
    for slot in range(capacity):
        parent = parent_ref[first + slot]
        parts = []
        for group in range(groups):
            low = (slot * groups + group) * per_group
            values = cache_ref[parent, 1, group]
            value_row = new_ref[
                0, slot, head_count + groups + group : head_count + groups + group + 1, :
            ]
            mixed = jnp.dot(
                weight[low : low + per_group], values, preferred_element_type=jnp.float32
            )
            mixed = mixed + newest_weight[low : low + per_group] * value_row.astype(jnp.float32)
            parts.append(mixed)
        out_ref[0, slot] = jnp.concatenate(parts, axis=0).astype(jnp.bfloat16)


def attend(parents, lengths, arrived, cache, head_count):
    device_count, capacity, rows, _ = arrived.shape
    spec = pltpu.PrefetchScalarGridSpec(
        num_scalar_prefetch=2,
        grid=(device_count,),
        in_specs=[
            pl.BlockSpec((1, capacity, rows, HEAD_DIM), lambda i, *_: (i, 0, 0, 0)),
            pl.BlockSpec(memory_space=pltpu.VMEM),
        ],
        out_specs=pl.BlockSpec((1, capacity, head_count, HEAD_DIM), lambda i, *_: (i, 0, 0, 0)),
    )
    return pl.pallas_call(
        functools.partial(attend_kernel, capacity, head_count),
        grid_spec=spec,
        out_shape=jax.ShapeDtypeStruct(
            (device_count, capacity, head_count, HEAD_DIM), jnp.bfloat16
        ),
        compiler_params=pltpu.CompilerParams(vmem_limit_bytes=40 * 1024 * 1024),
        name="attend",
    )(parents, lengths, arrived, cache)


MESH = pl.DeviceIdType.MESH


def remote(src, dst, send_sem, recv_sem, device):
    return pltpu.make_async_remote_copy(
        src_ref=src,
        dst_ref=dst,
        send_sem=send_sem,
        recv_sem=recv_sem,
        device_id=device,
        device_id_type=MESH,
    )


def greet(devices):
    barrier = pltpu.get_barrier_semaphore()
    for device in devices:
        pl.semaphore_signal(barrier, inc=1, device_id=device, device_id_type=MESH)
    pl.semaphore_wait(barrier, len(devices))


def scatter_sum(chunk, high, low, partner, peers, bufs):
    product, half, got, block, landed, sems = bufs
    half_send, half_recv, block_send, block_recv = sems
    half[chunk] = product[chunk, :, 1 - low].astype(jnp.bfloat16)
    first = remote(
        half.at[chunk], got.at[chunk], half_send.at[chunk], half_recv.at[chunk], partner
    )
    first.start()

    def second():
        first.wait()
        copies = []
        for step, peer in enumerate(peers):
            other = lax.rem(high + step + 1, len(peers) + 1)
            block[chunk, step] = (
                product[chunk, other, low] + got[chunk, other].astype(jnp.float32)
            ).astype(jnp.bfloat16)
            copy = remote(
                block.at[chunk, step],
                landed.at[chunk, step],
                block_send.at[chunk, step],
                block_recv.at[chunk, step],
                peer,
            )
            copy.start()
            copies.append(copy)

        def finish():
            for copy in copies:
                copy.wait()
            total = product[chunk, high, low] + got[chunk, high].astype(jnp.float32)
            for step in range(len(peers)):
                total = total + landed[chunk, step].astype(jnp.float32)
            return total

        return finish

    return second


def project_kernel(
    n,
    hidden_ref,
    gain_ref,
    query_ref,
    key_ref,
    value_ref,
    cosine_ref,
    sine_ref,
    placing_ref,
    cache_ref,
    out_ref,
    sorted_ref,
    hidden_own,
    query_own,
    tail_own,
    raw,
    packed,
    arrive,
    load_sems,
    slot_send,
    slot_recv,
    blocks,
    product,
    half,
    got,
    block,
    landed,
    move_send,
    move_recv,
    pass_send,
    pass_recv,
    half_send,
    half_recv,
    block_send,
    block_recv,
):
    me = lax.axis_index("dp")
    rank = lax.axis_index("tensor")
    core = lax.rem(rank, 2)
    capacity = placing_ref.shape[0] // n
    twin = (me, rank + 1 - 2 * core)
    high, low = me // 2, lax.rem(me, 2)
    partner = (me + 1 - 2 * low, rank)
    peers = [(lax.rem(high + d, n // 2) * 2 + low, rank) for d in range(1, n // 2)]
    others = [(lax.rem(me + d, n), rank) for d in range(1, n)]
    rows, depth = hidden_ref.shape[0], query_ref.shape[0]
    part = rows // 2
    key_width = key_ref.shape[1]
    loads = [
        pltpu.make_async_copy(source, target, load_sems.at[at])
        for at, (source, target) in enumerate(
            [
                (hidden_ref, hidden_own),
                (cache_ref, raw),
                (query_ref, query_own),
                (key_ref, tail_own.at[:, :key_width]),
                (value_ref, tail_own.at[:, key_width:]),
            ]
        )
    ]
    for load in loads:
        load.start()
    greet(others + [twin])
    mine = pl.ds(pl.multiple_of(core * part, part), part)
    theirs = pl.ds(pl.multiple_of((1 - core) * part, part), part)
    moves = []
    for d in range(1, n):
        target = lax.rem(me + d, n)
        columns = pl.ds(pl.multiple_of(target * depth, depth), depth)
        copy = remote(
            hidden_ref.at[mine, columns],
            blocks.at[d, mine],
            move_send.at[d],
            move_recv.at[d],
            (target, rank),
        )
        copy.start()
        moves.append(copy)
    loads[0].wait()
    blocks[0] = hidden_own[:, pl.ds(pl.multiple_of(me * depth, depth), depth)]
    hidden = hidden_own[...].astype(jnp.float32)
    inverse = lax.rsqrt(
        jnp.sum(hidden * hidden, axis=1, keepdims=True) / hidden_ref.shape[1] + 1e-06
    )
    loads[1].wait()
    kinds = 2 * sorted_ref.shape[2]
    span = 256
    each = span // kinds
    to = lax.broadcasted_iota(jnp.int32, (span, span), 0)
    of = lax.broadcasted_iota(jnp.int32, (span, span), 1)
    order = (of == kinds * (to % each) + to // each).astype(jnp.bfloat16)

    def sort_beam(beam, carry):
        for piece in range(raw.shape[1] // span):
            moved = jnp.dot(
                order,
                raw[beam, piece * span : (piece + 1) * span, :],
                preferred_element_type=jnp.float32,
            ).astype(jnp.bfloat16)
            for kind in range(kinds):
                sorted_ref[
                    beam,
                    kind // sorted_ref.shape[2],
                    kind % sorted_ref.shape[2],
                    piece * each : (piece + 1) * each,
                    :,
                ] = moved[kind * each : (kind + 1) * each]
        return carry

    lax.fori_loop(0, raw.shape[0], sort_beam, 0)
    passes = []
    for d in range(1, n):
        moves[d - 1].wait_recv()
        copy = remote(
            blocks.at[d, mine], blocks.at[d, mine], pass_send.at[d], pass_recv.at[d], twin
        )
        copy.start()
        passes.append(copy)
    for d in range(1, n):
        moves[d - 1].wait_send()
        passes[d - 1].wait_send()
        remote(
            blocks.at[d, theirs], blocks.at[d, theirs], pass_send.at[d], pass_recv.at[d], twin
        ).wait_recv()
    gain = gain_ref[...].astype(jnp.float32)
    scaled = jnp.concatenate(
        [(blocks[d].astype(jnp.float32) * gain).astype(jnp.bfloat16) for d in range(n)], axis=0
    )
    width = product.shape[-1]
    chunks = product.shape[0]
    bufs = (product, half, got, block, landed, (half_send, half_recv, block_send, block_recv))
    seconds = []
    for load in loads[2:]:
        load.wait()
    for chunk in range(chunks):
        if chunk < chunks - 1:
            weight = query_own[:, chunk * width : (chunk + 1) * width]
        else:
            weight = tail_own[...]
        result = jnp.dot(scaled, weight, preferred_element_type=jnp.float32)
        for d in range(n):
            owner = lax.rem(me - d + n, n)
            product[chunk, owner // 2, lax.rem(owner, 2)] = result[d * rows : (d + 1) * rows]
        seconds.append(scatter_sum(chunk, high, low, partner, peers, bufs))
    finishes = [second() for second in seconds]
    cosine, sine = cosine_ref[...], sine_ref[...]
    for chunk in range(chunks):
        total = finishes[chunk]() * inverse
        for first in range(0, width, HEAD_DIM):
            vector = total[:, first : first + HEAD_DIM]
            if chunk < chunks - 1 or first < width // 2:
                vector = vector * cosine + pltpu.roll(vector, HEAD_DIM // 2, 1) * sine
            at = chunk * width + first
            vector = jnp.dot(
                placing_ref[...], vector.astype(jnp.bfloat16), preferred_element_type=jnp.float32
            )
            for d in range(n):
                packed[d, :, at : at + HEAD_DIM] = vector[
                    d * capacity : (d + 1) * capacity
                ].astype(jnp.bfloat16)
    copies = []
    for d in range(1, n):
        target = lax.rem(me + d, n)
        copy = remote(
            packed.at[target], arrive.at[me], slot_send.at[d], slot_recv.at[d], (target, rank)
        )
        copy.start()
        copies.append(copy)
    arrive[me] = packed[me]
    for copy in copies:
        copy.wait_send()
    for d in range(1, n):
        source = lax.rem(me - d + n, n)
        remote(
            packed.at[source], arrive.at[source], slot_send.at[d], slot_recv.at[d], (source, rank)
        ).wait_recv()
    out_ref[...] = arrive[...]


def sum_scratch(chunks, nh, rows, width):
    return [
        pltpu.VMEM((chunks, nh, 2, rows, width), jnp.float32),
        pltpu.VMEM((chunks, nh, rows, width), jnp.bfloat16),
        pltpu.VMEM((chunks, nh, rows, width), jnp.bfloat16),
        pltpu.VMEM((chunks, max(nh - 1, 1), rows, width), jnp.bfloat16),
        pltpu.VMEM((chunks, max(nh - 1, 1), rows, width), jnp.bfloat16),
    ]


def sum_sems(chunks, nh):
    return [
        pltpu.SemaphoreType.DMA((chunks,)),
        pltpu.SemaphoreType.DMA((chunks,)),
        pltpu.SemaphoreType.DMA((chunks, max(nh - 1, 1))),
        pltpu.SemaphoreType.DMA((chunks, max(nh - 1, 1))),
    ]


def project(
    n, hidden, gain, query_weight, key_weight, value_weight, cosine, sine, placing, cache
):
    rows = hidden.shape[0]
    depth, query_width = query_weight.shape
    width = 2 * key_weight.shape[1]
    chunks = query_width // width + 1
    capacity = placing.shape[0] // n
    beams, length, _, groups, _ = cache.shape
    flat = cache.reshape(beams, length * 2 * groups, HEAD_DIM)
    vmem = pl.BlockSpec(memory_space=pltpu.VMEM)
    hbm = pl.BlockSpec(memory_space=pl.ANY)
    return pl.pallas_call(
        functools.partial(project_kernel, n),
        out_shape=[
            jax.ShapeDtypeStruct((n, capacity, chunks * width), jnp.bfloat16),
            jax.ShapeDtypeStruct((beams, 2, groups, length, HEAD_DIM), jnp.bfloat16),
        ],
        in_specs=[hbm, vmem, hbm, hbm, hbm, vmem, vmem, vmem, hbm],
        out_specs=[vmem, vmem],
        scratch_shapes=[
            pltpu.VMEM(hidden.shape, jnp.bfloat16),
            pltpu.VMEM(query_weight.shape, jnp.bfloat16),
            pltpu.VMEM((depth, width), jnp.bfloat16),
            pltpu.VMEM(flat.shape, jnp.bfloat16),
            pltpu.VMEM((n, capacity, chunks * width), jnp.bfloat16),
            pltpu.VMEM((n, capacity, chunks * width), jnp.bfloat16),
            pltpu.SemaphoreType.DMA((5,)),
            pltpu.SemaphoreType.DMA((n,)),
            pltpu.SemaphoreType.DMA((n,)),
            pltpu.VMEM((n, rows, depth), jnp.bfloat16),
        ]
        + sum_scratch(chunks, n // 2, rows, width)
        + [pltpu.SemaphoreType.DMA((n,))] * 4
        + sum_sems(chunks, n // 2),
        compiler_params=pltpu.CompilerParams(
            collective_id=0, has_side_effects=True, vmem_limit_bytes=56 * 1024 * 1024
        ),
        cost_estimate=pl.CostEstimate(
            flops=2 * n * rows * depth * chunks * width, bytes_accessed=8000000, transcendentals=0
        ),
        name="project",
    )(hidden, gain, query_weight, key_weight, value_weight, cosine, sine, placing, flat)


def output_kernel(
    n,
    ranks,
    slots_ref,
    picking_ref,
    weight_ref,
    out_ref,
    weight_own,
    back,
    mixed_ref,
    load_sem,
    slot_send,
    slot_recv,
    gathered,
    whole,
    product,
    half,
    got,
    block,
    landed,
    own_send,
    pass_send,
    take_recv,
    end_send,
    end_pass,
    end_recv,
    half_send,
    half_recv,
    block_send,
    block_recv,
):
    me = lax.axis_index("dp")
    rank = lax.axis_index("tensor")
    high, low = me // 2, lax.rem(me, 2)
    partner = (me + 1 - 2 * low, rank)
    nh = n // 2
    row_peers = [(lax.rem(high + d, nh) * 2 + low, rank) for d in range(1, nh)]
    x, core = rank // 2, lax.rem(rank, 2)
    twin = (me, rank + 1 - 2 * core)
    nx = ranks // 2
    x_peers = [(me, lax.rem(x + d, nx) * 2 + core) for d in range(1, nx)]
    load = pltpu.make_async_copy(weight_ref, weight_own, load_sem.at[0])
    load.start()
    greet([twin] + x_peers + [(lax.rem(me + d, n), rank) for d in range(1, n)])
    copies = []
    for d in range(1, n):
        target = lax.rem(me + d, n)
        copy = remote(
            slots_ref.at[target], back.at[me], slot_send.at[d], slot_recv.at[d], (target, rank)
        )
        copy.start()
        copies.append(copy)
    back[me] = slots_ref[me]
    for d in range(1, n):
        source = lax.rem(me - d + n, n)
        remote(
            slots_ref.at[source], back.at[source], slot_send.at[d], slot_recv.at[d], (source, rank)
        ).wait_recv()
    held = jnp.concatenate([back[d].astype(jnp.float32) for d in range(n)], axis=0)
    mixed_ref[...] = jnp.dot(
        picking_ref[...], held.astype(jnp.bfloat16), preferred_element_type=jnp.float32
    ).astype(jnp.bfloat16)
    for copy in copies:
        copy.wait_send()

    sends = []
    for d, peer in enumerate([partner] + row_peers):
        copy = remote(mixed_ref, gathered.at[me], own_send.at[d], take_recv.at[me], peer)
        copy.start()
        sends.append(copy)
    gathered[me] = mixed_ref[...]
    for d in range(1, nh):
        source = lax.rem(high - d + nh, nh) * 2 + low
        spot = gathered.at[source]
        remote(spot, spot, own_send.at[d], take_recv.at[source], partner).wait_recv()
        copy = remote(spot, spot, pass_send.at[d], take_recv.at[source], partner)
        copy.start()
        sends.append(copy)
    for d in range(nh):
        source = lax.rem(high - d + nh, nh) * 2 + 1 - low
        spot = gathered.at[source]
        remote(spot, spot, own_send.at[0], take_recv.at[source], partner).wait_recv()
    for copy in sends:
        copy.wait_send()

    rows, width = product.shape[3], product.shape[4]
    chunks = product.shape[0]
    load.wait()
    everything = gathered[...].reshape(n * mixed_ref.shape[0], mixed_ref.shape[1])
    bufs = (product, half, got, block, landed, (half_send, half_recv, block_send, block_recv))
    seconds = []
    for chunk in range(chunks):
        result = jnp.dot(
            everything,
            weight_own[:, chunk * width : (chunk + 1) * width],
            preferred_element_type=jnp.float32,
        )
        for place in range(ranks):
            product[chunk, place // 2, place % 2] = result[place * rows : (place + 1) * rows]
        seconds.append(scatter_sum(chunk, x, core, twin, x_peers, bufs))
    finishes = [second() for second in seconds]
    sends = []
    for chunk in range(chunks):
        whole[chunk, rank] = finishes[chunk]().astype(jnp.bfloat16)
        spot = whole.at[chunk, rank]
        for d, peer in enumerate([twin] + x_peers):
            copy = remote(spot, spot, end_send.at[chunk, d], end_recv.at[chunk, rank], peer)
            copy.start()
            sends.append(copy)
    for chunk in range(chunks):
        for d in range(1, nx):
            source = lax.rem(x - d + nx, nx) * 2 + core
            spot = whole.at[chunk, source]
            remote(
                spot, spot, end_send.at[chunk, d], end_recv.at[chunk, source], twin
            ).wait_recv()
            copy = remote(
                spot, spot, end_pass.at[chunk, d], end_recv.at[chunk, source], twin
            )
            copy.start()
            sends.append(copy)
    for chunk in range(chunks):
        for d in range(nx):
            source = lax.rem(x - d + nx, nx) * 2 + 1 - core
            spot = whole.at[chunk, source]
            remote(
                spot, spot, end_send.at[chunk, 0], end_recv.at[chunk, source], twin
            ).wait_recv()
    for copy in sends:
        copy.wait_send()
    for chunk in range(chunks):
        for place in range(ranks):
            out_ref[place * rows : (place + 1) * rows, chunk * width : (chunk + 1) * width] = whole[
                chunk, place
            ]


def output(n, ranks, slots, picking, weight):
    depth = slots.shape[2]
    local = picking.shape[0]
    columns = weight.shape[1]
    width = min(256, columns)
    chunks = columns // width
    rows = n * local // ranks
    vmem = pl.BlockSpec(memory_space=pltpu.VMEM)
    return pl.pallas_call(
        functools.partial(output_kernel, n, ranks),
        out_shape=jax.ShapeDtypeStruct((n * local, columns), jnp.bfloat16),
        in_specs=[vmem, vmem, pl.BlockSpec(memory_space=pl.ANY)],
        out_specs=vmem,
        scratch_shapes=[
            pltpu.VMEM(weight.shape, jnp.bfloat16),
            pltpu.VMEM(slots.shape, jnp.bfloat16),
            pltpu.VMEM((local, depth), jnp.bfloat16),
            pltpu.SemaphoreType.DMA((1,)),
            pltpu.SemaphoreType.DMA((n,)),
            pltpu.SemaphoreType.DMA((n,)),
            pltpu.VMEM((n, local, depth), jnp.bfloat16),
            pltpu.VMEM((chunks, ranks, rows, width), jnp.bfloat16),
        ]
        + sum_scratch(chunks, ranks // 2, rows, width)
        + [pltpu.SemaphoreType.DMA((n,))] * 3
        + [pltpu.SemaphoreType.DMA((chunks, ranks))] * 3
        + sum_sems(chunks, ranks // 2),
        compiler_params=pltpu.CompilerParams(
            collective_id=1, has_side_effects=True, vmem_limit_bytes=56 * 1024 * 1024
        ),
        cost_estimate=pl.CostEstimate(
            flops=2 * n * local * depth * columns, bytes_accessed=8000000, transcendentals=0
        ),
        name="output",
    )(slots, picking, weight)


def arrival_ranks(sources):
    ordinal = jnp.arange(sources.shape[-1], dtype=jnp.int32)
    earlier = (sources[..., None, :] == sources[..., :, None]) & (
        ordinal[None, :] < ordinal[:, None]
    )
    return jnp.sum(earlier.astype(jnp.int32), axis=-1)


def body(
    hidden_in,
    norm_gain,
    query_weight,
    key_weight,
    value_weight,
    output_weight,
    key_value_cache,
    cache_lengths,
    parent_beam,
    beam_alive,
):
    device_count = lax.axis_size("dp")
    device_rank = lax.axis_index("dp")
    local_beams = hidden_in.shape[0]
    capacity = max(2, (2 * local_beams + device_count - 1) // device_count)
    slot_total = device_count * capacity
    query_width = query_weight.shape[1]
    key_width = key_weight.shape[1]
    head_count = query_width // HEAD_DIM
    group_count = key_width // HEAD_DIM
    row_count = head_count + 2 * group_count

    all_parents = parent_beam.reshape(device_count, local_beams)
    all_sources = all_parents // local_beams
    all_ranks = arrival_ranks(all_sources)
    beam_index = jnp.arange(parent_beam.shape[0], dtype=jnp.int32)
    all_positions = jnp.sum(
        jnp.where(parent_beam[:, None] == beam_index[None, :], cache_lengths[None, :], 0), axis=1
    )
    held = (all_sources == device_rank)[:, None, :] & (
        all_ranks[:, None, :] == jnp.arange(capacity, dtype=jnp.int32)[None, :, None]
    )
    slot_parent = jnp.sum(jnp.where(held, (all_parents % local_beams)[:, None, :], 0), axis=2)
    slot_length = jnp.sum(
        jnp.where(held, all_positions.reshape(device_count, 1, local_beams), 0), axis=2
    )

    first_beam = device_rank * local_beams
    my_alive = lax.dynamic_slice_in_dim(beam_alive, first_beam, local_beams)
    position = lax.dynamic_slice_in_dim(all_positions, first_beam, local_beams)
    my_source = lax.dynamic_slice_in_dim(all_sources, device_rank, 1)[0]
    my_rank = lax.dynamic_slice_in_dim(all_ranks, device_rank, 1)[0]
    target = my_source * capacity + my_rank
    placing = (jnp.arange(slot_total, dtype=jnp.int32)[:, None] == target[None, :]).astype(
        jnp.bfloat16
    )
    picking = (
        (jnp.arange(slot_total, dtype=jnp.int32)[None, :] == target[:, None])
        & (my_alive[:, None] > 0)
    ).astype(jnp.bfloat16)

    cosine, sine = turn_angles(position)
    arrived, cache = project(
        device_count,
        hidden_in,
        norm_gain[None, :],
        query_weight,
        key_weight,
        value_weight,
        cosine,
        sine,
        placing,
        key_value_cache,
    )
    arrived = arrived.reshape(device_count, capacity, row_count, HEAD_DIM)
    mixed = attend(
        slot_parent.reshape(-1), slot_length.reshape(-1), arrived, cache, head_count
    )
    slots = mixed.reshape(device_count, capacity, query_width)
    return output(device_count, lax.axis_size("tensor"), slots, picking, output_weight)


def solution(mesh):
    placed = (
        P("dp", None),
        P("dp"),
        P("dp", "tensor"),
        P("dp", "tensor"),
        P("dp", "tensor"),
        P("tensor", "dp"),
        P("dp", None, None, "tensor", None),
        P(),
        P(),
        P(),
    )
    return jax.shard_map(body, mesh=mesh, in_specs=placed, out_specs=P(None, "dp"), check_vma=False)
```

```python
import functools
import math

import jax
import jax.numpy as jnp
from jax import lax
from jax.experimental import pallas as pl
from jax.experimental.pallas import tpu as pltpu
from jax.sharding import PartitionSpec as P

HEAD_DIM = 128


def turn_angles(position):
    half_width = HEAD_DIM // 2
    pair_index = jnp.arange(half_width).astype(jnp.float32)
    frequency = jnp.exp(pair_index * (-2.0 * math.log(1000000.0) / HEAD_DIM))
    angles = position.astype(jnp.float32)[:, None] * frequency[None, :]
    cosine, sine = jnp.cos(angles), jnp.sin(angles)
    return (
        jnp.concatenate([cosine, cosine], axis=1),
        jnp.concatenate([-sine, sine], axis=1),
    )


def attend_kernel(capacity, head_count, parent_ref, length_ref, new_ref, *refs):
    caches, out_ref = refs[:capacity], refs[capacity]
    groups = caches[0].shape[2]
    per_group = head_count // groups
    first = pl.program_id(0) * capacity
    score_scale = 1.0 / math.sqrt(HEAD_DIM)
    rows = groups * per_group
    scores, latest, limits = [], [], []
    for slot in range(capacity):
        limits.append(jnp.full((rows, 1), length_ref[first + slot], jnp.int32))
        for group in range(groups):
            query = new_ref[0, slot, group * per_group : (group + 1) * per_group, :]
            key_row = new_ref[0, slot, head_count + group : head_count + group + 1, :]
            keys = caches[slot][0, 0, group]
            scores.append(
                lax.dot_general(
                    query, keys, (((1,), (1,)), ((), ())), preferred_element_type=jnp.float32
                )
            )
            latest.append(
                jnp.sum(
                    query.astype(jnp.float32) * key_row.astype(jnp.float32), axis=1, keepdims=True
                )
            )
    cached = jnp.concatenate(scores, axis=0) * score_scale
    newest = jnp.concatenate(latest, axis=0) * score_scale
    limit = jnp.concatenate(limits, axis=0)
    slots = lax.broadcasted_iota(jnp.int32, cached.shape, 1)
    cached = jnp.where(slots < limit, cached, -jnp.inf)
    highest = jnp.maximum(jnp.max(cached, axis=1, keepdims=True), newest)
    cached_exp = jnp.exp(cached - highest)
    newest_exp = jnp.exp(newest - highest)
    denominator = jnp.sum(cached_exp, axis=1, keepdims=True) + newest_exp
    weight = (cached_exp / denominator).astype(jnp.bfloat16)
    newest_weight = (newest_exp / denominator).astype(jnp.bfloat16).astype(jnp.float32)
    for slot in range(capacity):
        parts = []
        for group in range(groups):
            low = (slot * groups + group) * per_group
            values = caches[slot][0, 1, group]
            value_row = new_ref[
                0, slot, head_count + groups + group : head_count + groups + group + 1, :
            ]
            mixed = jnp.dot(
                weight[low : low + per_group], values, preferred_element_type=jnp.float32
            )
            mixed = mixed + newest_weight[low : low + per_group] * value_row.astype(jnp.float32)
            parts.append(mixed)
        out_ref[0, slot] = jnp.concatenate(parts, axis=0).astype(jnp.bfloat16)


def attend(parents, lengths, arrived, cache, head_count):
    device_count, capacity, rows, _ = arrived.shape
    spec = pltpu.PrefetchScalarGridSpec(
        num_scalar_prefetch=2,
        grid=(device_count,),
        in_specs=[
            pl.BlockSpec((1, capacity, rows, HEAD_DIM), lambda i, *_: (i, 0, 0, 0)),
        ]
        + [
            pl.BlockSpec(
                (1,) + cache.shape[1:],
                lambda i, parents, _, slot=slot: (parents[i * capacity + slot], 0, 0, 0, 0),
            )
            for slot in range(capacity)
        ],
        out_specs=pl.BlockSpec((1, capacity, head_count, HEAD_DIM), lambda i, *_: (i, 0, 0, 0)),
    )
    return pl.pallas_call(
        functools.partial(attend_kernel, capacity, head_count),
        grid_spec=spec,
        out_shape=jax.ShapeDtypeStruct(
            (device_count, capacity, head_count, HEAD_DIM), jnp.bfloat16
        ),
        compiler_params=pltpu.CompilerParams(vmem_limit_bytes=56 * 1024 * 1024),
        name="attend",
    )(parents, lengths, arrived, *[cache] * capacity)


MESH = pl.DeviceIdType.MESH


def remote(src, dst, send_sem, recv_sem, device):
    return pltpu.make_async_remote_copy(
        src_ref=src,
        dst_ref=dst,
        send_sem=send_sem,
        recv_sem=recv_sem,
        device_id=device,
        device_id_type=MESH,
    )


def greet(devices):
    barrier = pltpu.get_barrier_semaphore()
    for device in devices:
        pl.semaphore_signal(barrier, inc=1, device_id=device, device_id_type=MESH)
    pl.semaphore_wait(barrier, len(devices))


def scatter_sum(chunk, high, low, partner, peers, bufs):
    product, half, got, block, landed, sems = bufs
    half_send, half_recv, block_send, block_recv = sems
    half[chunk] = product[chunk, :, 1 - low].astype(jnp.bfloat16)
    first = remote(
        half.at[chunk], got.at[chunk], half_send.at[chunk], half_recv.at[chunk], partner
    )
    first.start()

    def second():
        first.wait()
        copies = []
        for step, peer in enumerate(peers):
            other = lax.rem(high + step + 1, len(peers) + 1)
            block[chunk, step] = (
                product[chunk, other, low] + got[chunk, other].astype(jnp.float32)
            ).astype(jnp.bfloat16)
            copy = remote(
                block.at[chunk, step],
                landed.at[chunk, step],
                block_send.at[chunk, step],
                block_recv.at[chunk, step],
                peer,
            )
            copy.start()
            copies.append(copy)

        def finish():
            for copy in copies:
                copy.wait()
            total = product[chunk, high, low] + got[chunk, high].astype(jnp.float32)
            for step in range(len(peers)):
                total = total + landed[chunk, step].astype(jnp.float32)
            return total

        return finish

    return second


def project_kernel(
    n,
    hidden_ref,
    gain_ref,
    query_ref,
    key_ref,
    value_ref,
    cosine_ref,
    sine_ref,
    placing_ref,
    cache_ref,
    out_ref,
    sorted_ref,
    hidden_own,
    query_own,
    tail_own,
    raw,
    packed,
    arrive,
    ordered,
    load_sems,
    store_sems,
    slot_send,
    slot_recv,
    blocks,
    product,
    half,
    got,
    block,
    landed,
    move_send,
    move_recv,
    pass_send,
    pass_recv,
    half_send,
    half_recv,
    block_send,
    block_recv,
):
    me = lax.axis_index("dp")
    rank = lax.axis_index("tensor")
    core = lax.rem(rank, 2)
    capacity = placing_ref.shape[0] // n
    twin = (me, rank + 1 - 2 * core)
    high, low = me // 2, lax.rem(me, 2)
    partner = (me + 1 - 2 * low, rank)
    peers = [(lax.rem(high + d, n // 2) * 2 + low, rank) for d in range(1, n // 2)]
    others = [(lax.rem(me + d, n), rank) for d in range(1, n)]
    rows, depth = hidden_ref.shape[0], query_ref.shape[0]
    part = rows // 2
    key_width = key_ref.shape[1]
    loads = [
        pltpu.make_async_copy(source, target, load_sems.at[at])
        for at, (source, target) in enumerate(
            [
                (hidden_ref, hidden_own),
                (cache_ref, raw),
                (query_ref, query_own),
                (key_ref, tail_own.at[:, :key_width]),
                (value_ref, tail_own.at[:, key_width:]),
            ]
        )
    ]
    for load in loads:
        load.start()
    greet(others + [twin])
    mine = pl.ds(pl.multiple_of(core * part, part), part)
    theirs = pl.ds(pl.multiple_of((1 - core) * part, part), part)
    moves = []
    for d in range(1, n):
        target = lax.rem(me + d, n)
        columns = pl.ds(pl.multiple_of(target * depth, depth), depth)
        copy = remote(
            hidden_ref.at[mine, columns],
            blocks.at[d, mine],
            move_send.at[d],
            move_recv.at[d],
            (target, rank),
        )
        copy.start()
        moves.append(copy)
    loads[0].wait()
    blocks[0] = hidden_own[:, pl.ds(pl.multiple_of(me * depth, depth), depth)]
    hidden = hidden_own[...].astype(jnp.float32)
    inverse = lax.rsqrt(
        jnp.sum(hidden * hidden, axis=1, keepdims=True) / hidden_ref.shape[1] + 1e-06
    )
    loads[1].wait()
    kinds = 2 * sorted_ref.shape[2]
    span = 256
    each = span // kinds
    to = lax.broadcasted_iota(jnp.int32, (span, span), 0)
    of = lax.broadcasted_iota(jnp.int32, (span, span), 1)
    order = (of == kinds * (to % each) + to // each).astype(jnp.bfloat16)

    def sort_beam(beam, carry):
        for piece in range(raw.shape[1] // span):
            moved = jnp.dot(
                order,
                raw[beam, piece * span : (piece + 1) * span, :],
                preferred_element_type=jnp.float32,
            ).astype(jnp.bfloat16)
            for kind in range(kinds):
                ordered[
                    beam,
                    kind // sorted_ref.shape[2],
                    kind % sorted_ref.shape[2],
                    piece * each : (piece + 1) * each,
                    :,
                ] = moved[kind * each : (kind + 1) * each]
        return carry

    beams, chunks = raw.shape[0], product.shape[0]
    cuts = [0, beams * 5 // 16]
    cuts += [cuts[1] + (step + 1) * (beams // 2) // chunks for step in range(chunks)]
    cuts += [beams]
    stores = []

    def sort_part(part):
        first, last = cuts[part], cuts[part + 1]
        lax.fori_loop(first, last, sort_beam, 0)
        store = pltpu.make_async_copy(
            ordered.at[first:last], sorted_ref.at[first:last], store_sems.at[part]
        )
        store.start()
        stores.append(store)

    sort_part(0)
    passes = []
    for d in range(1, n):
        moves[d - 1].wait_recv()
        copy = remote(
            blocks.at[d, mine], blocks.at[d, mine], pass_send.at[d], pass_recv.at[d], twin
        )
        copy.start()
        passes.append(copy)
    for d in range(1, n):
        moves[d - 1].wait_send()
        passes[d - 1].wait_send()
        remote(
            blocks.at[d, theirs], blocks.at[d, theirs], pass_send.at[d], pass_recv.at[d], twin
        ).wait_recv()
    gain = gain_ref[...].astype(jnp.float32)
    scaled = jnp.concatenate(
        [(blocks[d].astype(jnp.float32) * gain).astype(jnp.bfloat16) for d in range(n)], axis=0
    )
    width = product.shape[-1]
    bufs = (product, half, got, block, landed, (half_send, half_recv, block_send, block_recv))
    seconds = []
    for load in loads[2:]:
        load.wait()
    for chunk in range(chunks):
        if chunk < chunks - 1:
            weight = query_own[:, chunk * width : (chunk + 1) * width]
        else:
            weight = tail_own[...]
        result = jnp.dot(scaled, weight, preferred_element_type=jnp.float32)
        for d in range(n):
            owner = lax.rem(me - d + n, n)
            product[chunk, owner // 2, lax.rem(owner, 2)] = result[d * rows : (d + 1) * rows]
        seconds.append(scatter_sum(chunk, high, low, partner, peers, bufs))
    finishes = []
    for chunk in range(chunks):
        sort_part(chunk + 1)
        finishes.append(seconds[chunk]())
    cosine, sine = cosine_ref[...], sine_ref[...]
    for chunk in range(chunks):
        total = finishes[chunk]() * inverse
        for first in range(0, width, HEAD_DIM):
            vector = total[:, first : first + HEAD_DIM]
            if chunk < chunks - 1 or first < width // 2:
                vector = vector * cosine + pltpu.roll(vector, HEAD_DIM // 2, 1) * sine
            at = chunk * width + first
            vector = jnp.dot(
                placing_ref[...], vector.astype(jnp.bfloat16), preferred_element_type=jnp.float32
            )
            for d in range(n):
                packed[d, :, at : at + HEAD_DIM] = vector[
                    d * capacity : (d + 1) * capacity
                ].astype(jnp.bfloat16)
    copies = []
    for d in range(1, n):
        target = lax.rem(me + d, n)
        copy = remote(
            packed.at[target], arrive.at[me], slot_send.at[d], slot_recv.at[d], (target, rank)
        )
        copy.start()
        copies.append(copy)
    arrive[me] = packed[me]
    sort_part(chunks + 1)
    for copy in copies:
        copy.wait_send()
    for d in range(1, n):
        source = lax.rem(me - d + n, n)
        remote(
            packed.at[source], arrive.at[source], slot_send.at[d], slot_recv.at[d], (source, rank)
        ).wait_recv()
    out_ref[...] = arrive[...]
    for store in stores:
        store.wait()


def sum_scratch(chunks, nh, rows, width):
    return [
        pltpu.VMEM((chunks, nh, 2, rows, width), jnp.float32),
        pltpu.VMEM((chunks, nh, rows, width), jnp.bfloat16),
        pltpu.VMEM((chunks, nh, rows, width), jnp.bfloat16),
        pltpu.VMEM((chunks, max(nh - 1, 1), rows, width), jnp.bfloat16),
        pltpu.VMEM((chunks, max(nh - 1, 1), rows, width), jnp.bfloat16),
    ]


def sum_sems(chunks, nh):
    return [
        pltpu.SemaphoreType.DMA((chunks,)),
        pltpu.SemaphoreType.DMA((chunks,)),
        pltpu.SemaphoreType.DMA((chunks, max(nh - 1, 1))),
        pltpu.SemaphoreType.DMA((chunks, max(nh - 1, 1))),
    ]


def project(
    n, hidden, gain, query_weight, key_weight, value_weight, cosine, sine, placing, cache
):
    rows = hidden.shape[0]
    depth, query_width = query_weight.shape
    width = 2 * key_weight.shape[1]
    chunks = query_width // width + 1
    capacity = placing.shape[0] // n
    beams, length, _, groups, _ = cache.shape
    flat = cache.reshape(beams, length * 2 * groups, HEAD_DIM)
    vmem = pl.BlockSpec(memory_space=pltpu.VMEM)
    hbm = pl.BlockSpec(memory_space=pl.ANY)
    return pl.pallas_call(
        functools.partial(project_kernel, n),
        out_shape=[
            jax.ShapeDtypeStruct((n, capacity, chunks * width), jnp.bfloat16),
            jax.ShapeDtypeStruct((beams, 2, groups, length, HEAD_DIM), jnp.bfloat16),
        ],
        in_specs=[hbm, vmem, hbm, hbm, hbm, vmem, vmem, vmem, hbm],
        out_specs=[vmem, hbm],
        scratch_shapes=[
            pltpu.VMEM(hidden.shape, jnp.bfloat16),
            pltpu.VMEM(query_weight.shape, jnp.bfloat16),
            pltpu.VMEM((depth, width), jnp.bfloat16),
            pltpu.VMEM(flat.shape, jnp.bfloat16),
            pltpu.VMEM((n, capacity, chunks * width), jnp.bfloat16),
            pltpu.VMEM((n, capacity, chunks * width), jnp.bfloat16),
            pltpu.VMEM((beams, 2, groups, length, HEAD_DIM), jnp.bfloat16),
            pltpu.SemaphoreType.DMA((5,)),
            pltpu.SemaphoreType.DMA((chunks + 2,)),
            pltpu.SemaphoreType.DMA((n,)),
            pltpu.SemaphoreType.DMA((n,)),
            pltpu.VMEM((n, rows, depth), jnp.bfloat16),
        ]
        + sum_scratch(chunks, n // 2, rows, width)
        + [pltpu.SemaphoreType.DMA((n,))] * 4
        + sum_sems(chunks, n // 2),
        compiler_params=pltpu.CompilerParams(
            collective_id=0, has_side_effects=True, vmem_limit_bytes=56 * 1024 * 1024
        ),
        cost_estimate=pl.CostEstimate(
            flops=2 * n * rows * depth * chunks * width, bytes_accessed=8000000, transcendentals=0
        ),
        name="project",
    )(hidden, gain, query_weight, key_weight, value_weight, cosine, sine, placing, flat)


def output_kernel(
    n,
    ranks,
    slots_ref,
    picking_ref,
    weight_ref,
    out_ref,
    weight_own,
    back,
    mixed_ref,
    load_sem,
    slot_send,
    slot_recv,
    gathered,
    whole,
    product,
    half,
    got,
    block,
    landed,
    own_send,
    pass_send,
    take_recv,
    end_send,
    end_pass,
    end_recv,
    half_send,
    half_recv,
    block_send,
    block_recv,
):
    me = lax.axis_index("dp")
    rank = lax.axis_index("tensor")
    high, low = me // 2, lax.rem(me, 2)
    partner = (me + 1 - 2 * low, rank)
    nh = n // 2
    row_peers = [(lax.rem(high + d, nh) * 2 + low, rank) for d in range(1, nh)]
    x, core = rank // 2, lax.rem(rank, 2)
    twin = (me, rank + 1 - 2 * core)
    nx = ranks // 2
    x_peers = [(me, lax.rem(x + d, nx) * 2 + core) for d in range(1, nx)]
    load = pltpu.make_async_copy(weight_ref, weight_own, load_sem.at[0])
    load.start()
    greet([twin] + x_peers + [(lax.rem(me + d, n), rank) for d in range(1, n)])
    copies = []
    for d in range(1, n):
        target = lax.rem(me + d, n)
        copy = remote(
            slots_ref.at[target], back.at[me], slot_send.at[d], slot_recv.at[d], (target, rank)
        )
        copy.start()
        copies.append(copy)
    back[me] = slots_ref[me]
    for d in range(1, n):
        source = lax.rem(me - d + n, n)
        remote(
            slots_ref.at[source], back.at[source], slot_send.at[d], slot_recv.at[d], (source, rank)
        ).wait_recv()
    held = jnp.concatenate([back[d].astype(jnp.float32) for d in range(n)], axis=0)
    mixed_ref[...] = jnp.dot(
        picking_ref[...], held.astype(jnp.bfloat16), preferred_element_type=jnp.float32
    ).astype(jnp.bfloat16)
    for copy in copies:
        copy.wait_send()

    sends = []
    for d, peer in enumerate([partner] + row_peers):
        copy = remote(mixed_ref, gathered.at[me], own_send.at[d], take_recv.at[me], peer)
        copy.start()
        sends.append(copy)
    gathered[me] = mixed_ref[...]
    for d in range(1, nh):
        source = lax.rem(high - d + nh, nh) * 2 + low
        spot = gathered.at[source]
        remote(spot, spot, own_send.at[d], take_recv.at[source], partner).wait_recv()
        copy = remote(spot, spot, pass_send.at[d], take_recv.at[source], partner)
        copy.start()
        sends.append(copy)
    for d in range(nh):
        source = lax.rem(high - d + nh, nh) * 2 + 1 - low
        spot = gathered.at[source]
        remote(spot, spot, own_send.at[0], take_recv.at[source], partner).wait_recv()
    for copy in sends:
        copy.wait_send()

    rows, width = product.shape[3], product.shape[4]
    chunks = product.shape[0]
    load.wait()
    everything = gathered[...].reshape(n * mixed_ref.shape[0], mixed_ref.shape[1])
    bufs = (product, half, got, block, landed, (half_send, half_recv, block_send, block_recv))
    seconds = []
    for chunk in range(chunks):
        result = jnp.dot(
            everything,
            weight_own[:, chunk * width : (chunk + 1) * width],
            preferred_element_type=jnp.float32,
        )
        for place in range(ranks):
            product[chunk, place // 2, place % 2] = result[place * rows : (place + 1) * rows]
        seconds.append(scatter_sum(chunk, x, core, twin, x_peers, bufs))
    finishes = [second() for second in seconds]
    sends = []
    for chunk in range(chunks):
        whole[chunk, rank] = finishes[chunk]().astype(jnp.bfloat16)
        spot = whole.at[chunk, rank]
        for d, peer in enumerate([twin] + x_peers):
            copy = remote(spot, spot, end_send.at[chunk, d], end_recv.at[chunk, rank], peer)
            copy.start()
            sends.append(copy)
    for chunk in range(chunks):
        for d in range(1, nx):
            source = lax.rem(x - d + nx, nx) * 2 + core
            spot = whole.at[chunk, source]
            remote(
                spot, spot, end_send.at[chunk, d], end_recv.at[chunk, source], twin
            ).wait_recv()
            copy = remote(
                spot, spot, end_pass.at[chunk, d], end_recv.at[chunk, source], twin
            )
            copy.start()
            sends.append(copy)
    for chunk in range(chunks):
        for d in range(nx):
            source = lax.rem(x - d + nx, nx) * 2 + 1 - core
            spot = whole.at[chunk, source]
            remote(
                spot, spot, end_send.at[chunk, 0], end_recv.at[chunk, source], twin
            ).wait_recv()
    for copy in sends:
        copy.wait_send()
    for chunk in range(chunks):
        for place in range(ranks):
            out_ref[place * rows : (place + 1) * rows, chunk * width : (chunk + 1) * width] = whole[
                chunk, place
            ]


def output(n, ranks, slots, picking, weight):
    depth = slots.shape[2]
    local = picking.shape[0]
    columns = weight.shape[1]
    width = min(256, columns)
    chunks = columns // width
    rows = n * local // ranks
    vmem = pl.BlockSpec(memory_space=pltpu.VMEM)
    return pl.pallas_call(
        functools.partial(output_kernel, n, ranks),
        out_shape=jax.ShapeDtypeStruct((n * local, columns), jnp.bfloat16),
        in_specs=[vmem, vmem, pl.BlockSpec(memory_space=pl.ANY)],
        out_specs=vmem,
        scratch_shapes=[
            pltpu.VMEM(weight.shape, jnp.bfloat16),
            pltpu.VMEM(slots.shape, jnp.bfloat16),
            pltpu.VMEM((local, depth), jnp.bfloat16),
            pltpu.SemaphoreType.DMA((1,)),
            pltpu.SemaphoreType.DMA((n,)),
            pltpu.SemaphoreType.DMA((n,)),
            pltpu.VMEM((n, local, depth), jnp.bfloat16),
            pltpu.VMEM((chunks, ranks, rows, width), jnp.bfloat16),
        ]
        + sum_scratch(chunks, ranks // 2, rows, width)
        + [pltpu.SemaphoreType.DMA((n,))] * 3
        + [pltpu.SemaphoreType.DMA((chunks, ranks))] * 3
        + sum_sems(chunks, ranks // 2),
        compiler_params=pltpu.CompilerParams(
            collective_id=1, has_side_effects=True, vmem_limit_bytes=56 * 1024 * 1024
        ),
        cost_estimate=pl.CostEstimate(
            flops=2 * n * local * depth * columns, bytes_accessed=8000000, transcendentals=0
        ),
        name="output",
    )(slots, picking, weight)


def arrival_ranks(sources):
    ordinal = jnp.arange(sources.shape[-1], dtype=jnp.int32)
    earlier = (sources[..., None, :] == sources[..., :, None]) & (
        ordinal[None, :] < ordinal[:, None]
    )
    return jnp.sum(earlier.astype(jnp.int32), axis=-1)


def body(
    hidden_in,
    norm_gain,
    query_weight,
    key_weight,
    value_weight,
    output_weight,
    key_value_cache,
    cache_lengths,
    parent_beam,
    beam_alive,
):
    device_count = lax.axis_size("dp")
    device_rank = lax.axis_index("dp")
    local_beams = hidden_in.shape[0]
    capacity = max(2, (2 * local_beams + device_count - 1) // device_count)
    slot_total = device_count * capacity
    query_width = query_weight.shape[1]
    key_width = key_weight.shape[1]
    head_count = query_width // HEAD_DIM
    group_count = key_width // HEAD_DIM
    row_count = head_count + 2 * group_count

    all_parents = parent_beam.reshape(device_count, local_beams)
    all_sources = all_parents // local_beams
    all_ranks = arrival_ranks(all_sources)
    beam_index = jnp.arange(parent_beam.shape[0], dtype=jnp.int32)
    all_positions = jnp.sum(
        jnp.where(parent_beam[:, None] == beam_index[None, :], cache_lengths[None, :], 0), axis=1
    )
    held = (all_sources == device_rank)[:, None, :] & (
        all_ranks[:, None, :] == jnp.arange(capacity, dtype=jnp.int32)[None, :, None]
    )
    slot_parent = jnp.sum(jnp.where(held, (all_parents % local_beams)[:, None, :], 0), axis=2)
    slot_length = jnp.sum(
        jnp.where(held, all_positions.reshape(device_count, 1, local_beams), 0), axis=2
    )

    first_beam = device_rank * local_beams
    my_alive = lax.dynamic_slice_in_dim(beam_alive, first_beam, local_beams)
    position = lax.dynamic_slice_in_dim(all_positions, first_beam, local_beams)
    my_source = lax.dynamic_slice_in_dim(all_sources, device_rank, 1)[0]
    my_rank = lax.dynamic_slice_in_dim(all_ranks, device_rank, 1)[0]
    target = my_source * capacity + my_rank
    placing = (jnp.arange(slot_total, dtype=jnp.int32)[:, None] == target[None, :]).astype(
        jnp.bfloat16
    )
    picking = (
        (jnp.arange(slot_total, dtype=jnp.int32)[None, :] == target[:, None])
        & (my_alive[:, None] > 0)
    ).astype(jnp.bfloat16)

    cosine, sine = turn_angles(position)
    arrived, cache = project(
        device_count,
        hidden_in,
        norm_gain[None, :],
        query_weight,
        key_weight,
        value_weight,
        cosine,
        sine,
        placing,
        key_value_cache,
    )
    arrived = arrived.reshape(device_count, capacity, row_count, HEAD_DIM)
    mixed = attend(
        slot_parent.reshape(-1), slot_length.reshape(-1), arrived, cache, head_count
    )
    slots = mixed.reshape(device_count, capacity, query_width)
    return output(device_count, lax.axis_size("tensor"), slots, picking, output_weight)


def solution(mesh):
    placed = (
        P("dp", None),
        P("dp"),
        P("dp", "tensor"),
        P("dp", "tensor"),
        P("dp", "tensor"),
        P("tensor", "dp"),
        P("dp", None, None, "tensor", None),
        P(),
        P(),
        P(),
    )
    return jax.shard_map(body, mesh=mesh, in_specs=placed, out_specs=P(None, "dp"), check_vma=False)
```

```python
import functools
import math

import jax
import jax.numpy as jnp
from jax import lax
from jax.experimental import pallas as pl
from jax.experimental.pallas import tpu as pltpu
from jax.sharding import PartitionSpec as P

HEAD_DIM = 128


def turn_angles(position):
    half_width = HEAD_DIM // 2
    pair_index = jnp.arange(half_width).astype(jnp.float32)
    frequency = jnp.exp(pair_index * (-2.0 * math.log(1000000.0) / HEAD_DIM))
    angles = position.astype(jnp.float32)[:, None] * frequency[None, :]
    cosine, sine = jnp.cos(angles), jnp.sin(angles)
    return (
        jnp.concatenate([cosine, cosine], axis=1),
        jnp.concatenate([-sine, sine], axis=1),
    )


def attend_kernel(capacity, head_count, parent_ref, length_ref, new_ref, cache_ref, out_ref):
    groups = cache_ref.shape[2]
    length = cache_ref.shape[3]
    per_group = head_count // groups
    first = pl.program_id(0) * capacity
    score_scale = 1.0 / math.sqrt(HEAD_DIM)
    rows = groups * per_group
    scores, latest, limits = [], [], []
    for slot in range(capacity):
        parent = parent_ref[first + slot]
        limits.append(jnp.full((rows, 1), length_ref[first + slot], jnp.int32))
        for group in range(groups):
            query = new_ref[0, slot, group * per_group : (group + 1) * per_group, :]
            key_row = new_ref[0, slot, head_count + group : head_count + group + 1, :]
            keys = cache_ref[parent, 0, group]
            scores.append(
                lax.dot_general(
                    query, keys, (((1,), (1,)), ((), ())), preferred_element_type=jnp.float32
                )
            )
            latest.append(
                jnp.sum(
                    query.astype(jnp.float32) * key_row.astype(jnp.float32), axis=1, keepdims=True
                )
            )
    cached = jnp.concatenate(scores, axis=0) * score_scale
    newest = jnp.concatenate(latest, axis=0) * score_scale
    limit = jnp.concatenate(limits, axis=0)
    slots = lax.broadcasted_iota(jnp.int32, cached.shape, 1)
    cached = jnp.where(slots < limit, cached, -jnp.inf)
    highest = jnp.maximum(jnp.max(cached, axis=1, keepdims=True), newest)
    cached_exp = jnp.exp(cached - highest)
    newest_exp = jnp.exp(newest - highest)
    denominator = jnp.sum(cached_exp, axis=1, keepdims=True) + newest_exp
    weight = (cached_exp / denominator).astype(jnp.bfloat16)
    newest_weight = (newest_exp / denominator).astype(jnp.bfloat16).astype(jnp.float32)
    for slot in range(capacity):
        parent = parent_ref[first + slot]
        parts = []
        for group in range(groups):
            low = (slot * groups + group) * per_group
            values = cache_ref[parent, 1, group]
            value_row = new_ref[
                0, slot, head_count + groups + group : head_count + groups + group + 1, :
            ]
            mixed = jnp.dot(
                weight[low : low + per_group], values, preferred_element_type=jnp.float32
            )
            mixed = mixed + newest_weight[low : low + per_group] * value_row.astype(jnp.float32)
            parts.append(mixed)
        out_ref[0, slot] = jnp.concatenate(parts, axis=0).astype(jnp.bfloat16)


def attend(parents, lengths, arrived, cache, head_count):
    device_count, capacity, rows, _ = arrived.shape
    spec = pltpu.PrefetchScalarGridSpec(
        num_scalar_prefetch=2,
        grid=(device_count,),
        in_specs=[
            pl.BlockSpec((1, capacity, rows, HEAD_DIM), lambda i, *_: (i, 0, 0, 0)),
            pl.BlockSpec(memory_space=pltpu.VMEM),
        ],
        out_specs=pl.BlockSpec((1, capacity, head_count, HEAD_DIM), lambda i, *_: (i, 0, 0, 0)),
    )
    return pl.pallas_call(
        functools.partial(attend_kernel, capacity, head_count),
        grid_spec=spec,
        out_shape=jax.ShapeDtypeStruct(
            (device_count, capacity, head_count, HEAD_DIM), jnp.bfloat16
        ),
        compiler_params=pltpu.CompilerParams(vmem_limit_bytes=40 * 1024 * 1024),
        name="attend",
    )(parents, lengths, arrived, cache)


MESH = pl.DeviceIdType.MESH


def remote(src, dst, send_sem, recv_sem, device):
    return pltpu.make_async_remote_copy(
        src_ref=src,
        dst_ref=dst,
        send_sem=send_sem,
        recv_sem=recv_sem,
        device_id=device,
        device_id_type=MESH,
    )


def greet(devices):
    barrier = pltpu.get_barrier_semaphore()
    for device in devices:
        pl.semaphore_signal(barrier, inc=1, device_id=device, device_id_type=MESH)
    pl.semaphore_wait(barrier, len(devices))


def scatter_sum(chunk, high, low, partner, peers, bufs):
    product, half, got, block, landed, sems = bufs
    half_send, half_recv, block_send, block_recv = sems
    half[chunk] = product[chunk, :, 1 - low].astype(jnp.bfloat16)
    first = remote(
        half.at[chunk], got.at[chunk], half_send.at[chunk], half_recv.at[chunk], partner
    )
    first.start()

    def second():
        first.wait()
        copies = []
        for step, peer in enumerate(peers):
            other = lax.rem(high + step + 1, len(peers) + 1)
            block[chunk, step] = (
                product[chunk, other, low] + got[chunk, other].astype(jnp.float32)
            ).astype(jnp.bfloat16)
            copy = remote(
                block.at[chunk, step],
                landed.at[chunk, step],
                block_send.at[chunk, step],
                block_recv.at[chunk, step],
                peer,
            )
            copy.start()
            copies.append(copy)

        def finish():
            for copy in copies:
                copy.wait()
            total = product[chunk, high, low] + got[chunk, high].astype(jnp.float32)
            for step in range(len(peers)):
                total = total + landed[chunk, step].astype(jnp.float32)
            return total

        return finish

    return second


def project_kernel(
    n,
    hidden_ref,
    gain_ref,
    query_ref,
    key_ref,
    value_ref,
    cosine_ref,
    sine_ref,
    placing_ref,
    cache_ref,
    out_ref,
    sorted_ref,
    hidden_own,
    query_own,
    tail_own,
    raw,
    packed,
    arrive,
    ordered,
    load_sems,
    store_sems,
    slot_send,
    slot_recv,
    blocks,
    product,
    half,
    got,
    block,
    landed,
    move_send,
    move_recv,
    pass_send,
    pass_recv,
    half_send,
    half_recv,
    block_send,
    block_recv,
):
    me = lax.axis_index("dp")
    rank = lax.axis_index("tensor")
    core = lax.rem(rank, 2)
    capacity = placing_ref.shape[0] // n
    twin = (me, rank + 1 - 2 * core)
    high, low = me // 2, lax.rem(me, 2)
    partner = (me + 1 - 2 * low, rank)
    peers = [(lax.rem(high + d, n // 2) * 2 + low, rank) for d in range(1, n // 2)]
    others = [(lax.rem(me + d, n), rank) for d in range(1, n)]
    rows, depth = hidden_ref.shape[0], query_ref.shape[0]
    part = rows // 2
    key_width = key_ref.shape[1]
    loads = [
        pltpu.make_async_copy(source, target, load_sems.at[at])
        for at, (source, target) in enumerate(
            [
                (hidden_ref, hidden_own),
                (cache_ref, raw),
                (query_ref, query_own),
                (key_ref, tail_own.at[:, :key_width]),
                (value_ref, tail_own.at[:, key_width:]),
            ]
        )
    ]
    for load in loads:
        load.start()
    greet(others + [twin])
    mine = pl.ds(pl.multiple_of(core * part, part), part)
    theirs = pl.ds(pl.multiple_of((1 - core) * part, part), part)
    moves = []
    for d in range(1, n):
        target = lax.rem(me + d, n)
        columns = pl.ds(pl.multiple_of(target * depth, depth), depth)
        copy = remote(
            hidden_ref.at[mine, columns],
            blocks.at[d, mine],
            move_send.at[d],
            move_recv.at[d],
            (target, rank),
        )
        copy.start()
        moves.append(copy)
    loads[0].wait()
    blocks[0] = hidden_own[:, pl.ds(pl.multiple_of(me * depth, depth), depth)]
    hidden = hidden_own[...].astype(jnp.float32)
    inverse = lax.rsqrt(
        jnp.sum(hidden * hidden, axis=1, keepdims=True) / hidden_ref.shape[1] + 1e-06
    )
    loads[1].wait()
    kinds = 2 * sorted_ref.shape[2]
    span = 256
    each = span // kinds
    to = lax.broadcasted_iota(jnp.int32, (span, span), 0)
    of = lax.broadcasted_iota(jnp.int32, (span, span), 1)
    order = (of == kinds * (to % each) + to // each).astype(jnp.bfloat16)

    def sort_beam(beam, carry):
        for piece in range(raw.shape[1] // span):
            moved = jnp.dot(
                order,
                raw[beam, piece * span : (piece + 1) * span, :],
                preferred_element_type=jnp.float32,
            ).astype(jnp.bfloat16)
            for kind in range(kinds):
                ordered[
                    beam,
                    kind // sorted_ref.shape[2],
                    kind % sorted_ref.shape[2],
                    piece * each : (piece + 1) * each,
                    :,
                ] = moved[kind * each : (kind + 1) * each]
        return carry

    beams, chunks = raw.shape[0], product.shape[0]
    cuts = [0, beams * 5 // 16]
    cuts += [cuts[1] + (step + 1) * (beams // 2) // chunks for step in range(chunks)]
    cuts += [beams]
    stores = []

    def sort_part(part):
        first, last = cuts[part], cuts[part + 1]
        lax.fori_loop(first, last, sort_beam, 0)
        store = pltpu.make_async_copy(
            ordered.at[first:last], sorted_ref.at[first:last], store_sems.at[part]
        )
        store.start()
        stores.append(store)

    sort_part(0)
    passes = []
    for d in range(1, n):
        moves[d - 1].wait_recv()
        copy = remote(
            blocks.at[d, mine], blocks.at[d, mine], pass_send.at[d], pass_recv.at[d], twin
        )
        copy.start()
        passes.append(copy)
    for d in range(1, n):
        moves[d - 1].wait_send()
        passes[d - 1].wait_send()
        remote(
            blocks.at[d, theirs], blocks.at[d, theirs], pass_send.at[d], pass_recv.at[d], twin
        ).wait_recv()
    gain = gain_ref[...].astype(jnp.float32)
    scaled = jnp.concatenate(
        [(blocks[d].astype(jnp.float32) * gain).astype(jnp.bfloat16) for d in range(n)], axis=0
    )
    width = product.shape[-1]
    bufs = (product, half, got, block, landed, (half_send, half_recv, block_send, block_recv))
    seconds = []
    for load in loads[2:]:
        load.wait()
    for chunk in range(chunks):
        if chunk < chunks - 1:
            weight = query_own[:, chunk * width : (chunk + 1) * width]
        else:
            weight = tail_own[...]
        result = jnp.dot(scaled, weight, preferred_element_type=jnp.float32)
        for d in range(n):
            owner = lax.rem(me - d + n, n)
            product[chunk, owner // 2, lax.rem(owner, 2)] = result[d * rows : (d + 1) * rows]
        seconds.append(scatter_sum(chunk, high, low, partner, peers, bufs))
    finishes = []
    for chunk in range(chunks):
        sort_part(chunk + 1)
        finishes.append(seconds[chunk]())
    cosine, sine = cosine_ref[...], sine_ref[...]
    for chunk in range(chunks):
        total = finishes[chunk]() * inverse
        for first in range(0, width, HEAD_DIM):
            vector = total[:, first : first + HEAD_DIM]
            if chunk < chunks - 1 or first < width // 2:
                vector = vector * cosine + pltpu.roll(vector, HEAD_DIM // 2, 1) * sine
            at = chunk * width + first
            vector = jnp.dot(
                placing_ref[...], vector.astype(jnp.bfloat16), preferred_element_type=jnp.float32
            )
            for d in range(n):
                packed[d, :, at : at + HEAD_DIM] = vector[
                    d * capacity : (d + 1) * capacity
                ].astype(jnp.bfloat16)
    copies = []
    for d in range(1, n):
        target = lax.rem(me + d, n)
        copy = remote(
            packed.at[target], arrive.at[me], slot_send.at[d], slot_recv.at[d], (target, rank)
        )
        copy.start()
        copies.append(copy)
    arrive[me] = packed[me]
    sort_part(chunks + 1)
    for copy in copies:
        copy.wait_send()
    for d in range(1, n):
        source = lax.rem(me - d + n, n)
        remote(
            packed.at[source], arrive.at[source], slot_send.at[d], slot_recv.at[d], (source, rank)
        ).wait_recv()
    out_ref[...] = arrive[...]
    for store in stores:
        store.wait()


def sum_scratch(chunks, nh, rows, width):
    return [
        pltpu.VMEM((chunks, nh, 2, rows, width), jnp.float32),
        pltpu.VMEM((chunks, nh, rows, width), jnp.bfloat16),
        pltpu.VMEM((chunks, nh, rows, width), jnp.bfloat16),
        pltpu.VMEM((chunks, max(nh - 1, 1), rows, width), jnp.bfloat16),
        pltpu.VMEM((chunks, max(nh - 1, 1), rows, width), jnp.bfloat16),
    ]


def sum_sems(chunks, nh):
    return [
        pltpu.SemaphoreType.DMA((chunks,)),
        pltpu.SemaphoreType.DMA((chunks,)),
        pltpu.SemaphoreType.DMA((chunks, max(nh - 1, 1))),
        pltpu.SemaphoreType.DMA((chunks, max(nh - 1, 1))),
    ]


def project(
    n, hidden, gain, query_weight, key_weight, value_weight, cosine, sine, placing, cache
):
    rows = hidden.shape[0]
    depth, query_width = query_weight.shape
    width = 2 * key_weight.shape[1]
    chunks = query_width // width + 1
    capacity = placing.shape[0] // n
    beams, length, _, groups, _ = cache.shape
    flat = cache.reshape(beams, length * 2 * groups, HEAD_DIM)
    vmem = pl.BlockSpec(memory_space=pltpu.VMEM)
    hbm = pl.BlockSpec(memory_space=pl.ANY)
    return pl.pallas_call(
        functools.partial(project_kernel, n),
        out_shape=[
            jax.ShapeDtypeStruct((n, capacity, chunks * width), jnp.bfloat16),
            jax.ShapeDtypeStruct((beams, 2, groups, length, HEAD_DIM), jnp.bfloat16),
        ],
        in_specs=[hbm, vmem, hbm, hbm, hbm, vmem, vmem, vmem, hbm],
        out_specs=[vmem, hbm],
        scratch_shapes=[
            pltpu.VMEM(hidden.shape, jnp.bfloat16),
            pltpu.VMEM(query_weight.shape, jnp.bfloat16),
            pltpu.VMEM((depth, width), jnp.bfloat16),
            pltpu.VMEM(flat.shape, jnp.bfloat16),
            pltpu.VMEM((n, capacity, chunks * width), jnp.bfloat16),
            pltpu.VMEM((n, capacity, chunks * width), jnp.bfloat16),
            pltpu.VMEM((beams, 2, groups, length, HEAD_DIM), jnp.bfloat16),
            pltpu.SemaphoreType.DMA((5,)),
            pltpu.SemaphoreType.DMA((chunks + 2,)),
            pltpu.SemaphoreType.DMA((n,)),
            pltpu.SemaphoreType.DMA((n,)),
            pltpu.VMEM((n, rows, depth), jnp.bfloat16),
        ]
        + sum_scratch(chunks, n // 2, rows, width)
        + [pltpu.SemaphoreType.DMA((n,))] * 4
        + sum_sems(chunks, n // 2),
        compiler_params=pltpu.CompilerParams(
            collective_id=0, has_side_effects=True, vmem_limit_bytes=56 * 1024 * 1024
        ),
        cost_estimate=pl.CostEstimate(
            flops=2 * n * rows * depth * chunks * width, bytes_accessed=8000000, transcendentals=0
        ),
        name="project",
    )(hidden, gain, query_weight, key_weight, value_weight, cosine, sine, placing, flat)


def output_kernel(
    n,
    ranks,
    slots_ref,
    picking_ref,
    weight_ref,
    out_ref,
    weight_own,
    back,
    mixed_ref,
    load_sem,
    slot_send,
    slot_recv,
    gathered,
    whole,
    product,
    half,
    got,
    block,
    landed,
    own_send,
    pass_send,
    take_recv,
    end_send,
    end_pass,
    end_recv,
    half_send,
    half_recv,
    block_send,
    block_recv,
):
    me = lax.axis_index("dp")
    rank = lax.axis_index("tensor")
    high, low = me // 2, lax.rem(me, 2)
    partner = (me + 1 - 2 * low, rank)
    nh = n // 2
    row_peers = [(lax.rem(high + d, nh) * 2 + low, rank) for d in range(1, nh)]
    x, core = rank // 2, lax.rem(rank, 2)
    twin = (me, rank + 1 - 2 * core)
    nx = ranks // 2
    x_peers = [(me, lax.rem(x + d, nx) * 2 + core) for d in range(1, nx)]
    load = pltpu.make_async_copy(weight_ref, weight_own, load_sem.at[0])
    load.start()
    greet([twin] + x_peers + [(lax.rem(me + d, n), rank) for d in range(1, n)])
    copies = []
    for d in range(1, n):
        target = lax.rem(me + d, n)
        copy = remote(
            slots_ref.at[target], back.at[me], slot_send.at[d], slot_recv.at[d], (target, rank)
        )
        copy.start()
        copies.append(copy)
    back[me] = slots_ref[me]
    for d in range(1, n):
        source = lax.rem(me - d + n, n)
        remote(
            slots_ref.at[source], back.at[source], slot_send.at[d], slot_recv.at[d], (source, rank)
        ).wait_recv()
    held = jnp.concatenate([back[d].astype(jnp.float32) for d in range(n)], axis=0)
    mixed_ref[...] = jnp.dot(
        picking_ref[...], held.astype(jnp.bfloat16), preferred_element_type=jnp.float32
    ).astype(jnp.bfloat16)
    for copy in copies:
        copy.wait_send()

    sends = []
    for d, peer in enumerate([partner] + row_peers):
        copy = remote(mixed_ref, gathered.at[me], own_send.at[d], take_recv.at[me], peer)
        copy.start()
        sends.append(copy)
    gathered[me] = mixed_ref[...]
    for d in range(1, nh):
        source = lax.rem(high - d + nh, nh) * 2 + low
        spot = gathered.at[source]
        remote(spot, spot, own_send.at[d], take_recv.at[source], partner).wait_recv()
        copy = remote(spot, spot, pass_send.at[d], take_recv.at[source], partner)
        copy.start()
        sends.append(copy)
    for d in range(nh):
        source = lax.rem(high - d + nh, nh) * 2 + 1 - low
        spot = gathered.at[source]
        remote(spot, spot, own_send.at[0], take_recv.at[source], partner).wait_recv()
    for copy in sends:
        copy.wait_send()

    rows, width = product.shape[3], product.shape[4]
    chunks = product.shape[0]
    load.wait()
    everything = gathered[...].reshape(n * mixed_ref.shape[0], mixed_ref.shape[1])
    bufs = (product, half, got, block, landed, (half_send, half_recv, block_send, block_recv))
    seconds = []
    for chunk in range(chunks):
        result = jnp.dot(
            everything,
            weight_own[:, chunk * width : (chunk + 1) * width],
            preferred_element_type=jnp.float32,
        )
        for place in range(ranks):
            product[chunk, place // 2, place % 2] = result[place * rows : (place + 1) * rows]
        seconds.append(scatter_sum(chunk, x, core, twin, x_peers, bufs))
    finishes = [second() for second in seconds]
    sends = []
    for chunk in range(chunks):
        whole[chunk, rank] = finishes[chunk]().astype(jnp.bfloat16)
        spot = whole.at[chunk, rank]
        for d, peer in enumerate([twin] + x_peers):
            copy = remote(spot, spot, end_send.at[chunk, d], end_recv.at[chunk, rank], peer)
            copy.start()
            sends.append(copy)
    for chunk in range(chunks):
        for d in range(1, nx):
            source = lax.rem(x - d + nx, nx) * 2 + core
            spot = whole.at[chunk, source]
            remote(
                spot, spot, end_send.at[chunk, d], end_recv.at[chunk, source], twin
            ).wait_recv()
            copy = remote(
                spot, spot, end_pass.at[chunk, d], end_recv.at[chunk, source], twin
            )
            copy.start()
            sends.append(copy)
    for chunk in range(chunks):
        for d in range(nx):
            source = lax.rem(x - d + nx, nx) * 2 + 1 - core
            spot = whole.at[chunk, source]
            remote(
                spot, spot, end_send.at[chunk, 0], end_recv.at[chunk, source], twin
            ).wait_recv()
    for copy in sends:
        copy.wait_send()
    for chunk in range(chunks):
        for place in range(ranks):
            out_ref[place * rows : (place + 1) * rows, chunk * width : (chunk + 1) * width] = whole[
                chunk, place
            ]


def output(n, ranks, slots, picking, weight):
    depth = slots.shape[2]
    local = picking.shape[0]
    columns = weight.shape[1]
    width = min(256, columns)
    chunks = columns // width
    rows = n * local // ranks
    vmem = pl.BlockSpec(memory_space=pltpu.VMEM)
    return pl.pallas_call(
        functools.partial(output_kernel, n, ranks),
        out_shape=jax.ShapeDtypeStruct((n * local, columns), jnp.bfloat16),
        in_specs=[vmem, vmem, pl.BlockSpec(memory_space=pl.ANY)],
        out_specs=vmem,
        scratch_shapes=[
            pltpu.VMEM(weight.shape, jnp.bfloat16),
            pltpu.VMEM(slots.shape, jnp.bfloat16),
            pltpu.VMEM((local, depth), jnp.bfloat16),
            pltpu.SemaphoreType.DMA((1,)),
            pltpu.SemaphoreType.DMA((n,)),
            pltpu.SemaphoreType.DMA((n,)),
            pltpu.VMEM((n, local, depth), jnp.bfloat16),
            pltpu.VMEM((chunks, ranks, rows, width), jnp.bfloat16),
        ]
        + sum_scratch(chunks, ranks // 2, rows, width)
        + [pltpu.SemaphoreType.DMA((n,))] * 3
        + [pltpu.SemaphoreType.DMA((chunks, ranks))] * 3
        + sum_sems(chunks, ranks // 2),
        compiler_params=pltpu.CompilerParams(
            collective_id=1, has_side_effects=True, vmem_limit_bytes=56 * 1024 * 1024
        ),
        cost_estimate=pl.CostEstimate(
            flops=2 * n * local * depth * columns, bytes_accessed=8000000, transcendentals=0
        ),
        name="output",
    )(slots, picking, weight)


def arrival_ranks(sources):
    ordinal = jnp.arange(sources.shape[-1], dtype=jnp.int32)
    earlier = (sources[..., None, :] == sources[..., :, None]) & (
        ordinal[None, :] < ordinal[:, None]
    )
    return jnp.sum(earlier.astype(jnp.int32), axis=-1)


def body(
    hidden_in,
    norm_gain,
    query_weight,
    key_weight,
    value_weight,
    output_weight,
    key_value_cache,
    cache_lengths,
    parent_beam,
    beam_alive,
):
    device_count = lax.axis_size("dp")
    device_rank = lax.axis_index("dp")
    local_beams = hidden_in.shape[0]
    capacity = max(2, (2 * local_beams + device_count - 1) // device_count)
    slot_total = device_count * capacity
    query_width = query_weight.shape[1]
    key_width = key_weight.shape[1]
    head_count = query_width // HEAD_DIM
    group_count = key_width // HEAD_DIM
    row_count = head_count + 2 * group_count

    all_parents = parent_beam.reshape(device_count, local_beams)
    all_sources = all_parents // local_beams
    all_ranks = arrival_ranks(all_sources)
    beam_index = jnp.arange(parent_beam.shape[0], dtype=jnp.int32)
    all_positions = jnp.sum(
        jnp.where(parent_beam[:, None] == beam_index[None, :], cache_lengths[None, :], 0), axis=1
    )
    held = (all_sources == device_rank)[:, None, :] & (
        all_ranks[:, None, :] == jnp.arange(capacity, dtype=jnp.int32)[None, :, None]
    )
    slot_parent = jnp.sum(jnp.where(held, (all_parents % local_beams)[:, None, :], 0), axis=2)
    slot_length = jnp.sum(
        jnp.where(held, all_positions.reshape(device_count, 1, local_beams), 0), axis=2
    )

    first_beam = device_rank * local_beams
    my_alive = lax.dynamic_slice_in_dim(beam_alive, first_beam, local_beams)
    position = lax.dynamic_slice_in_dim(all_positions, first_beam, local_beams)
    my_source = lax.dynamic_slice_in_dim(all_sources, device_rank, 1)[0]
    my_rank = lax.dynamic_slice_in_dim(all_ranks, device_rank, 1)[0]
    target = my_source * capacity + my_rank
    placing = (jnp.arange(slot_total, dtype=jnp.int32)[:, None] == target[None, :]).astype(
        jnp.bfloat16
    )
    picking = (
        (jnp.arange(slot_total, dtype=jnp.int32)[None, :] == target[:, None])
        & (my_alive[:, None] > 0)
    ).astype(jnp.bfloat16)

    cosine, sine = turn_angles(position)
    arrived, cache = project(
        device_count,
        hidden_in,
        norm_gain[None, :],
        query_weight,
        key_weight,
        value_weight,
        cosine,
        sine,
        placing,
        key_value_cache,
    )
    arrived = arrived.reshape(device_count, capacity, row_count, HEAD_DIM)
    mixed = attend(
        slot_parent.reshape(-1), slot_length.reshape(-1), arrived, cache, head_count
    )
    slots = mixed.reshape(device_count, capacity, query_width)
    return output(device_count, lax.axis_size("tensor"), slots, picking, output_weight)


def solution(mesh):
    placed = (
        P("dp", None),
        P("dp"),
        P("dp", "tensor"),
        P("dp", "tensor"),
        P("dp", "tensor"),
        P("tensor", "dp"),
        P("dp", None, None, "tensor", None),
        P(),
        P(),
        P(),
    )
    return jax.shard_map(body, mesh=mesh, in_specs=placed, out_specs=P(None, "dp"), check_vma=False)
```
